32 devices in a mesh: seq: 8 (over y, x, core), head: 4 (over z).
Axes of the slice: x: 2, y: 2, z: 4, core: 2. Of those that a mesh axis runs over, the one named last changes fastest.
Arguments:
- input_embeddings: bfloat16 [2048, 1024], P('seq'), may hold values from -6 to 6
- loss_adjoint: bfloat16 [2048, 1024], P('seq'), may hold values from -6 to 6
- earliest_tier_content: bfloat16 [2048, 1024], P('seq', 'head'), may hold values from -6 to 6
- opening_memory: float32 [2, 16, 64, 64], P(None, 'head'), may hold values from -4 to 4
- live_extents: int32 [2], replicated, may hold values from 513 to 1024, as said below
- lagged_blend_coeffs: float32 [7, 1024], replicated, may hold values from 0 to 1
- standardize_scales: float32 [2, 1024], replicated, may hold values from 0.25 to 1.75
- standardize_offsets: float32 [2, 1024], replicated, may hold values from -2 to 2
- adapter_narrowing_coeffs: float32 [1024, 288], replicated, may hold values from -0.1875 to 0.1875
- adapter_widening_coeffs: float32 [288, 1024], P(None, 'head'), may hold values from -0.75 to 0.75
- attention_scale_lines: float32 [3, 1024], P(None, 'head'), may hold values from 0.25 to 1.75
- attention_offset_lines: float32 [3, 1024], P(None, 'head'), may hold values from -4 to 4
- present_reward_array: float32 [1024], P('head'), may hold values from -3 to 3
- forgetting_offset: float32 [1024], P('head'), may hold values from -9.5 to 1.25
- readin_maps: float32 [3, 1024, 1024], P(None, None, 'head'), may hold values from -0.1875 to 0.1875
- emission_coeffs: float32 [1024, 1024], P('head'), may hold values from -0.1875 to 0.1875
- feedforward_address_coeffs: float32 [1024, 4096], P(None, 'head'), may hold values from -0.1875 to 0.1875
- feedforward_content_coeffs: float32 [4096, 1024], P('head'), may hold values from -0.09375 to 0.09375
- lagged_blend_velocity: float32 [7, 1024], replicated, may hold values from -12 to 12
- standardize_scale_velocity: float32 [2, 1024], replicated, may hold values from -30 to 30
- standardize_offset_velocity: float32 [2, 1024], replicated, may hold values from -36 to 36
- narrowing_velocity: float32 [1024, 288], replicated, may hold values from -4 to 4
- widening_velocity: float32 [288, 1024], P(None, 'head'), may hold values from -25 to 25
- attention_scale_velocity: float32 [3, 1024], P(None, 'head'), may hold values from -8 to 8
- attention_offset_velocity: float32 [3, 1024], P(None, 'head'), may hold values from -8 to 8
- reward_velocity_array: float32 [1024], P('head'), may hold values from -8 to 8
- forgetting_velocity: float32 [1024], P('head'), may hold values from -4 to 4
- readin_velocity: float32 [3, 1024, 1024], P(None, None, 'head'), may hold values from -15 to 15
- emission_velocity: float32 [1024, 1024], P('head'), may hold values from -15 to 15
- feedforward_address_velocity: float32 [1024, 4096], P(None, 'head'), may hold values from -20 to 20
- feedforward_content_velocity: float32 [4096, 1024], P('head'), may hold values from -20 to 20
Outputs:
- block_output: bfloat16 [2048, 1024], P('seq')
- tokens_grad: float32 [2048, 1024], P('seq')
- first_grad: float32 [2048, 1024], P('seq', 'head')
- state_grad: float32 [2, 16, 64, 64], P(None, 'head')
- next_shift: float32 [7, 1024], replicated
- next_gains: float32 [2, 1024], replicated
- next_biases: float32 [2, 1024], replicated
- next_down: float32 [1024, 288], replicated
- next_up: float32 [288, 1024], P(None, 'head')
- next_headgain: float32 [3, 1024], P(None, 'head')
- next_headbias: float32 [3, 1024], P(None, 'head')
- next_bonus: float32 [1024], P('head')
- next_decay: float32 [1024], P('head')
- next_project: float32 [3, 1024, 1024], P(None, 'seq', 'head')
- next_output: float32 [1024, 1024], P('head', 'seq')
- next_ffnkey: float32 [1024, 4096], P('seq', 'head')
- next_ffnvalue: float32 [4096, 1024], P('head', 'seq')
- momentum_shift: float32 [7, 1024], replicated
- momentum_gains: float32 [2, 1024], replicated
- momentum_biases: float32 [2, 1024], replicated
- momentum_down: float32 [1024, 288], replicated
- momentum_up: float32 [288, 1024], P(None, 'head')
- momentum_headgain: float32 [3, 1024], P(None, 'head')
- momentum_headbias: float32 [3, 1024], P(None, 'head')
- momentum_bonus: float32 [1024], P('head')
- momentum_decay: float32 [1024], P('head')
- momentum_project: float32 [3, 1024, 1024], P(None, None, 'head')
- momentum_output: float32 [1024, 1024], P('head')
- momentum_ffnkey: float32 [1024, 4096], P(None, 'head')
- momentum_ffnvalue: float32 [4096, 1024], P('head')
The draws below stay inside these ranges and needn't reach their ends.
Inputs may be any that keep to these rules, and one draw needn't show every extreme that they name: `live_extents`: in every draw some sequence has all 1024 slots live.
All inputs are finite; a program needn't handle non-finite values.
Results may differ from the reference program's by a relative error of at most 0.012.
The reference program's roundings to bfloat16 on the way count: a program that leaves them out, or rounds other values in their place, can miss the bound.
Values sent between devices are 32-bit elements; how exact they have to be, the bound alone decides.
A program may use at most 256 MiB of HBM per device.

```python
import math
import jax
import jax.numpy as jnp
from jax import lax

EMBED_SIZE = 1024
HEADS = 16
HEAD_SIZE = 64
FF = 4096
LOWRANK_DECAY = 64
LOWRANK_RATE = 64
LOWRANK_VALUE = 32
LOWRANK_GATE = 128
BLOCK = 64
NS_STEPS = 5
SEQS = 2
TOK_DEV = 256
LOWRANK_TOTAL = 288
PLACE_TALLY = 2048
SLOTS = 1024
N_SEQ = 8


def draw_live_extents(key, part):
    pick_key = jax.random.fold_in(key, 11)
    size_key = jax.random.fold_in(key, 12)
    drawn = jax.random.randint(size_key, (SEQS,), SLOTS // 2 + 1, SLOTS + 1)
    full = jax.random.randint(pick_key, (), 0, SEQS)
    return jnp.where(jnp.arange(SEQS) == full, SLOTS, drawn).astype(jnp.int32)


def draw_forgetting_offset(key, part):
    head_key = jax.random.fold_in(key, 21)
    channel_key = jax.random.fold_in(key, 22)
    base = jax.random.uniform(head_key, (HEADS, 1), jnp.float32, -8.5, 0.5)
    noise = jax.random.uniform(channel_key, (HEADS, HEAD_SIZE), jnp.float32, -0.75, 0.75)
    return (base + noise).reshape(EMBED_SIZE).astype(jnp.float32)


def ramped_normal(key, shape, dim, base_scale):
    ramp_top = 2.0
    position = lax.broadcasted_iota(jnp.float32, shape, dim) / shape[dim]
    noise = jax.random.truncated_normal(key, -4.0, 4.0, shape, jnp.float32)
    return (noise * base_scale * (1.0 + ramp_top * position)).astype(jnp.float32)


def draw_readin_velocity(key, part):
    return ramped_normal(jax.random.fold_in(key, 31), (3, EMBED_SIZE, EMBED_SIZE), 2, 0.75)


def draw_emission_velocity(key, part):
    return ramped_normal(jax.random.fold_in(key, 32), (EMBED_SIZE, EMBED_SIZE), 0, 0.75)


def draw_feedforward_address_velocity(key, part):
    return ramped_normal(jax.random.fold_in(key, 33), (EMBED_SIZE, FF), 1, 1.0)


def draw_feedforward_content_velocity(key, part):
    return ramped_normal(jax.random.fold_in(key, 34), (FF, EMBED_SIZE), 0, 1.0)


def draw_widening_velocity(key, part):
    return ramped_normal(jax.random.fold_in(key, 35), (LOWRANK_TOTAL, EMBED_SIZE), 1, 1.25)


def block_levels(stream_key, extent, shards, smallest, high):
    level, own = 1.0, jax.random.fold_in(stream_key, 6)
    for dim, parts in shards:
        heights = jnp.exp(jax.random.uniform(jax.random.fold_in(own, dim), (parts,), jnp.float32, smallest / len(shards), high / len(shards)))
        level = level * jnp.repeat(heights, extent[dim] // parts).reshape([-1 if axis == dim else 1 for axis in range(len(extent))])
    return level


def normal_values(stream_key, dims, scale, bound, shards=(), held_as=jnp.bfloat16):
    level = block_levels(stream_key, dims, shards, -0.22, 0.18) if shards else 1.0
    result = jax.random.normal(stream_key, dims, jnp.float32) * scale * level
    return jnp.minimum(jnp.maximum(result, -bound), bound).astype(held_as)


def setup_inputs(seed: int = 0) -> dict:
    splits = jax.random.split(jax.random.key(seed), 32)
    input_embeddings = normal_values(splits[0], (PLACE_TALLY, EMBED_SIZE), 1.0, 6.0, ((0, 8),))
    loss_adjoint = normal_values(splits[1], (PLACE_TALLY, EMBED_SIZE), 1.0, 6.0, ((0, 8),))
    earliest_tier_content = normal_values(splits[2], (PLACE_TALLY, EMBED_SIZE), 1.0, 6.0, ((0, 8), (1, 4)))
    opening_memory = normal_values(splits[3], (SEQS, HEADS, HEAD_SIZE, HEAD_SIZE), 0.5, 4.0, ((1, 4),), jnp.float32)
    live_extents = draw_live_extents(jax.random.fold_in(splits[31], 71), 0)
    lagged_blend_coeffs = jnp.clip(jax.random.uniform(splits[5], (7, EMBED_SIZE), jnp.float32, 0.0, 1.0), 0.0, 1.0)
    standardize_scales = jnp.clip(1.0 + 0.15 * jax.random.normal(splits[6], (2, EMBED_SIZE), jnp.float32), 0.25, 1.75)
    standardize_offsets = normal_values(splits[7], (2, EMBED_SIZE), 0.3, 2.0, (), jnp.float32)
    adapter_narrowing_coeffs = normal_values(splits[8], (EMBED_SIZE, LOWRANK_TOTAL), EMBED_SIZE ** -0.5, 0.1875, (), jnp.float32)
    adapter_widening_coeffs = normal_values(splits[9], (LOWRANK_TOTAL, EMBED_SIZE), LOWRANK_DECAY ** -0.5, 0.75, ((1, 4),), jnp.float32)
    attention_scale_lines = jnp.clip(1.0 + 0.15 * jax.random.normal(splits[10], (3, EMBED_SIZE), jnp.float32), 0.25, 1.75)
    attention_offset_lines = normal_values(splits[11], (3, EMBED_SIZE), 1.0, 4.0, ((1, 4),), jnp.float32)
    present_reward_array = normal_values(splits[12], (EMBED_SIZE,), 0.5, 3.0, ((0, 4),), jnp.float32)
    forgetting_offset = draw_forgetting_offset(jax.random.fold_in(splits[31], 71), 0)
    readin_maps = normal_values(splits[14], (3, EMBED_SIZE, EMBED_SIZE), EMBED_SIZE ** -0.5, 0.1875, ((2, 4),), jnp.float32)
    emission_coeffs = normal_values(splits[15], (EMBED_SIZE, EMBED_SIZE), EMBED_SIZE ** -0.5, 0.1875, ((0, 4),), jnp.float32)
    feedforward_address_coeffs = normal_values(splits[16], (EMBED_SIZE, FF), EMBED_SIZE ** -0.5, 0.1875, ((1, 4),), jnp.float32)
    feedforward_content_coeffs = normal_values(splits[17], (FF, EMBED_SIZE), FF ** -0.5, 0.09375, ((0, 4),), jnp.float32)
    lagged_blend_velocity = normal_values(splits[18], (7, EMBED_SIZE), 3.0, 12.0, (), jnp.float32)
    standardize_scale_velocity = normal_values(splits[19], (2, EMBED_SIZE), 7.5, 30.0, (), jnp.float32)
    standardize_offset_velocity = normal_values(splits[20], (2, EMBED_SIZE), 9.0, 36.0, (), jnp.float32)
    narrowing_velocity = normal_values(splits[21], (EMBED_SIZE, LOWRANK_TOTAL), 0.5, 4.0, (), jnp.float32)
    widening_velocity = draw_widening_velocity(jax.random.fold_in(splits[31], 71), 0)
    attention_scale_velocity = normal_values(splits[23], (3, EMBED_SIZE), 2.0, 8.0, ((1, 4),), jnp.float32)
    attention_offset_velocity = normal_values(splits[24], (3, EMBED_SIZE), 2.0, 8.0, ((1, 4),), jnp.float32)
    reward_velocity_array = normal_values(splits[25], (EMBED_SIZE,), 2.0, 8.0, ((0, 4),), jnp.float32)
    forgetting_velocity = normal_values(splits[26], (EMBED_SIZE,), 0.5, 4.0, ((0, 4),), jnp.float32)
    readin_velocity = draw_readin_velocity(jax.random.fold_in(splits[31], 71), 0)
    emission_velocity = draw_emission_velocity(jax.random.fold_in(splits[31], 71), 0)
    feedforward_address_velocity = draw_feedforward_address_velocity(jax.random.fold_in(splits[31], 71), 0)
    feedforward_content_velocity = draw_feedforward_content_velocity(jax.random.fold_in(splits[31], 71), 0)
    return {"input_embeddings": input_embeddings, "loss_adjoint": loss_adjoint, "earliest_tier_content": earliest_tier_content, "opening_memory": opening_memory, "live_extents": live_extents, "lagged_blend_coeffs": lagged_blend_coeffs, "standardize_scales": standardize_scales, "standardize_offsets": standardize_offsets, "adapter_narrowing_coeffs": adapter_narrowing_coeffs, "adapter_widening_coeffs": adapter_widening_coeffs, "attention_scale_lines": attention_scale_lines, "attention_offset_lines": attention_offset_lines, "present_reward_array": present_reward_array, "forgetting_offset": forgetting_offset, "readin_maps": readin_maps, "emission_coeffs": emission_coeffs, "feedforward_address_coeffs": feedforward_address_coeffs, "feedforward_content_coeffs": feedforward_content_coeffs, "lagged_blend_velocity": lagged_blend_velocity, "standardize_scale_velocity": standardize_scale_velocity, "standardize_offset_velocity": standardize_offset_velocity, "narrowing_velocity": narrowing_velocity, "widening_velocity": widening_velocity, "attention_scale_velocity": attention_scale_velocity, "attention_offset_velocity": attention_offset_velocity, "reward_velocity_array": reward_velocity_array, "forgetting_velocity": forgetting_velocity, "readin_velocity": readin_velocity, "emission_velocity": emission_velocity, "feedforward_address_velocity": feedforward_address_velocity, "feedforward_content_velocity": feedforward_content_velocity}


HIGHEST = lax.Precision.HIGHEST
COEFF_A = 3.4445
COEFF_B = -4.775
COEFF_C = 2.0315
ORTHO_STEP_RATE = 0.5
VECTOR_RATE = 0.75
DECAY_KEEP = 0.5

@jax.custom_vjp
def low(v):
    return lax.optimization_barrier(v.astype(jnp.bfloat16)).astype(jnp.float32)

@jax.custom_vjp
def low_back(v):
    return v

def low_keep(v):
    return (low(v), None)

def low_pass(kept, grad):
    return (grad,)

def back_keep(v):
    return (v, None)

def back_low(kept, grad):
    return (low(grad),)
low.defvjp(low_keep, low_pass)
low_back.defvjp(back_keep, back_low)

def matmul(left, right):
    return jnp.dot(left, right, precision=HIGHEST, preferred_element_type=jnp.float32)

def layer_norm(content_lines, gain, bias):
    centered = content_lines - lax.optimization_barrier(jnp.mean(content_lines, axis=-1, keepdims=True))
    variance = lax.optimization_barrier(jnp.mean(centered * centered, axis=-1, keepdims=True))
    return centered * lax.rsqrt(variance + 1e-05) * gain + bias

def to_sequences(item):
    grouped = item.reshape((N_SEQ // SEQS, SEQS, TOK_DEV) + item.shape[1:])
    return jnp.swapaxes(grouped, 0, 1).reshape((SEQS, SLOTS) + item.shape[1:])

def from_sequences(item):
    grouped = item.reshape((SEQS, N_SEQ // SEQS, TOK_DEV) + item.shape[2:])
    return jnp.swapaxes(grouped, 0, 1).reshape((PLACE_TALLY,) + item.shape[2:])

def previous_token(content_lines):
    clustered_lines = to_sequences(content_lines)
    moved_rows = jnp.concatenate([jnp.zeros_like(clustered_lines[:, :1]), clustered_lines[:, :-1]], axis=1)
    return from_sequences(moved_rows)

def token_step(carried_memory, inputs):
    acceptance_lines, log_decay, alpha, beta, address_lines, content_lines = inputs
    carried = jnp.einsum('hvk,hk->hv', carried_memory, alpha, precision=HIGHEST)
    carried_memory = carried_memory * jnp.exp(log_decay)[:, None, :] + carried[:, :, None] * beta[:, None, :] + content_lines[:, :, None] * address_lines[:, None, :]
    return (carried_memory, jnp.einsum('hvk,hk->hv', carried_memory, acceptance_lines, precision=HIGHEST))

def block_pass(carried_memory, block):
    return lax.scan(token_step, carried_memory, block)

def sequence_pass(carried_memory, residual_streams):
    blocks = tuple((item.reshape(SLOTS // BLOCK, BLOCK, HEADS, HEAD_SIZE) for item in residual_streams))
    carried_memory, outputs = lax.scan(jax.checkpoint(block_pass), carried_memory, blocks)
    return outputs.reshape(SLOTS, HEADS, HEAD_SIZE)

def attention_tally(item):
    return item.reshape(PLACE_TALLY, HEADS, HEAD_SIZE)

def spans_list():
    sequence_edges = (0, LOWRANK_DECAY, LOWRANK_DECAY + LOWRANK_RATE, LOWRANK_DECAY + LOWRANK_RATE + LOWRANK_VALUE, LOWRANK_DECAY + LOWRANK_RATE + LOWRANK_VALUE + LOWRANK_GATE)
    return list(zip(sequence_edges[:-1], sequence_edges[1:]))

def forward(learnable_tensors, input_embeddings, earliest_tier_content, opening_memory):
    lagged_blend_coeffs, standardize_scales, standardize_offsets, adapter_narrowing_coeffs, adapter_widening_coeffs, attention_scale_lines, attention_offset_lines, present_reward_array, forgetting_offset, readin_maps, emission_coeffs, feedforward_address_coeffs, feedforward_content_coeffs = learnable_tensors
    sequence_spans = spans_list()
    normed = layer_norm(input_embeddings, standardize_scales[0], standardize_offsets[0])
    delta = previous_token(normed) - normed
    mixed = [low(normed + delta * lagged_blend_coeffs[index]) for index in range(6)]
    acceptance_lines = low_back(matmul(mixed[0], low(readin_maps[0])))
    address_lines = low_back(matmul(mixed[2], low(readin_maps[1])))
    content_lines = low_back(matmul(mixed[3], low(readin_maps[2])))
    down_matrix = low(adapter_narrowing_coeffs)
    up_matrix = low(adapter_widening_coeffs)
    sources = (1, 4, 3, 5)
    hidden = [low_back(matmul(mixed[sources[index]], down_matrix[:, sequence_spans[index][0]:sequence_spans[index][1]])) for index in range(4)]
    acts = [low(jnp.tanh(hidden[0])), low(hidden[1]), low(hidden[2]), low(jax.nn.sigmoid(hidden[3]))]
    widened_lines = [low_back(matmul(acts[index], up_matrix[sequence_spans[index][0]:sequence_spans[index][1]])) for index in range(4)]
    log_decay = -jnp.exp(-jax.nn.softplus(-(forgetting_offset + widened_lines[0])) - 0.5)
    rate = jax.nn.sigmoid(attention_offset_lines[0] + widened_lines[1])
    content_lines = content_lines + (earliest_tier_content - content_lines) * jax.nn.sigmoid(attention_offset_lines[1] + widened_lines[2])
    scaled = attention_tally(address_lines * attention_scale_lines[0])
    unit = scaled * lax.rsqrt(lax.optimization_barrier(jnp.sum(scaled * scaled, axis=-1, keepdims=True)) + 1e-05)
    address_lines = address_lines * (1.0 + (rate - 1.0) * attention_scale_lines[1])
    residual_streams = (attention_tally(acceptance_lines), attention_tally(log_decay), -unit, unit * attention_tally(rate), attention_tally(address_lines), attention_tally(content_lines))
    residual_streams = tuple((to_sequences(item) for item in residual_streams))
    outputs = from_sequences(jax.vmap(sequence_pass)(opening_memory, residual_streams))
    centered = outputs - lax.optimization_barrier(jnp.mean(outputs, axis=-1, keepdims=True))
    variance = lax.optimization_barrier(jnp.mean(centered * centered, axis=-1, keepdims=True))
    clustered_lines = (centered * lax.rsqrt(variance + 0.00064)).reshape(PLACE_TALLY, EMBED_SIZE) * attention_scale_lines[2] + attention_offset_lines[2]
    reward_summand = lax.optimization_barrier(jnp.sum(attention_tally(acceptance_lines * address_lines * present_reward_array), axis=-1, keepdims=True)) * attention_tally(content_lines)
    adapter_result = low((clustered_lines + reward_summand.reshape(PLACE_TALLY, EMBED_SIZE)) * widened_lines[3])
    attended = input_embeddings + low_back(matmul(adapter_result, low(emission_coeffs)))
    normed_two = layer_norm(attended, standardize_scales[1], standardize_offsets[1])
    key_in = low(normed_two + (previous_token(normed_two) - normed_two) * lagged_blend_coeffs[6])
    hidden_ffn = low_back(matmul(key_in, low(feedforward_address_coeffs)))
    activated = low(jnp.square(jax.nn.relu(hidden_ffn)))
    return attended + low_back(matmul(activated, low(feedforward_content_coeffs)))

def orthogonal_update(matrix):
    current = matrix / (jnp.sqrt(jnp.sum(matrix * matrix)) + 1e-07)
    for step in range(NS_STEPS):
        gram = matmul(current, current.T)
        first = matmul(gram, current)
        second = matmul(gram, first)
        current = COEFF_A * current + COEFF_B * first + COEFF_C * second
    return current

def vector_step(param, moved_rows):
    blocks = moved_rows.reshape(moved_rows.shape[:-1] + (moved_rows.shape[-1] // HEAD_SIZE, HEAD_SIZE))
    scale = jnp.sqrt(lax.optimization_barrier(jnp.mean(blocks * blocks, axis=-1, keepdims=True))) + 1e-06
    return param - VECTOR_RATE * (blocks / scale).reshape(moved_rows.shape)

def reference(input_embeddings, loss_adjoint, earliest_tier_content, opening_memory, live_extents, lagged_blend_coeffs, standardize_scales, standardize_offsets, adapter_narrowing_coeffs, adapter_widening_coeffs, attention_scale_lines, attention_offset_lines, present_reward_array, forgetting_offset, readin_maps, emission_coeffs, feedforward_address_coeffs, feedforward_content_coeffs, lagged_blend_velocity, standardize_scale_velocity, standardize_offset_velocity, narrowing_velocity, widening_velocity, attention_scale_velocity, attention_offset_velocity, reward_velocity_array, forgetting_velocity, readin_velocity, emission_velocity, feedforward_address_velocity, feedforward_content_velocity):
    learnable_tensors = (lagged_blend_coeffs, standardize_scales, standardize_offsets, adapter_narrowing_coeffs, adapter_widening_coeffs, attention_scale_lines, attention_offset_lines, present_reward_array, forgetting_offset, readin_maps, emission_coeffs, feedforward_address_coeffs, feedforward_content_coeffs)
    velocity_collection = (lagged_blend_velocity, standardize_scale_velocity, standardize_offset_velocity, narrowing_velocity, widening_velocity, attention_scale_velocity, attention_offset_velocity, reward_velocity_array, forgetting_velocity, readin_velocity, emission_velocity, feedforward_address_velocity, feedforward_content_velocity)
    slot_ids = lax.broadcasted_iota(jnp.int32, (SEQS, SLOTS), 1)
    live_grid = (slot_ids < live_extents.astype(jnp.int32)[:, None]).astype(jnp.float32)
    live = from_sequences(live_grid[:, :, None])
    output, pullback = jax.vjp(forward, learnable_tensors, input_embeddings.astype(jnp.float32), earliest_tier_content.astype(jnp.float32), opening_memory)
    grads, tokens_grad, first_grad, state_grad = pullback(loss_adjoint.astype(jnp.float32) * live)
    block_output = (output * live).astype(jnp.bfloat16)
    moved_rows = [DECAY_KEEP * velocity + grad for velocity, grad in zip(velocity_collection, grads)]
    next_values = list(learnable_tensors)
    for index in (0, 1, 2, 5, 6, 7, 8):
        next_values[index] = vector_step(learnable_tensors[index], moved_rows[index])
    sequence_spans = spans_list()
    next_values[3] = adapter_narrowing_coeffs - ORTHO_STEP_RATE * jnp.concatenate([math.sqrt(max(1.0, EMBED_SIZE / (stop_index - start_index))) * orthogonal_update(moved_rows[3][:, start_index:stop_index].T).T for start_index, stop_index in sequence_spans], axis=1)
    next_values[4] = adapter_widening_coeffs - ORTHO_STEP_RATE * jnp.concatenate([orthogonal_update(moved_rows[4][start_index:stop_index]) for start_index, stop_index in sequence_spans], axis=0)
    next_values[9] = readin_maps - ORTHO_STEP_RATE * jnp.stack([orthogonal_update(moved_rows[9][index]) for index in range(3)])
    next_values[10] = emission_coeffs - ORTHO_STEP_RATE * orthogonal_update(moved_rows[10].T).T
    next_values[11] = feedforward_address_coeffs - ORTHO_STEP_RATE * orthogonal_update(moved_rows[11])
    next_values[12] = feedforward_content_coeffs - ORTHO_STEP_RATE * math.sqrt(max(1.0, FF / EMBED_SIZE)) * orthogonal_update(moved_rows[12].T).T
    return (block_output, tokens_grad, first_grad, state_grad, next_values[0], next_values[1], next_values[2], next_values[3], next_values[4], next_values[5], next_values[6], next_values[7], next_values[8], next_values[9], next_values[10], next_values[11], next_values[12], moved_rows[0], moved_rows[1], moved_rows[2], moved_rows[3], moved_rows[4], moved_rows[5], moved_rows[6], moved_rows[7], moved_rows[8], moved_rows[9], moved_rows[10], moved_rows[11], moved_rows[12])
```

```python
import functools
import math

import jax
import jax.numpy as jnp
from jax import lax
from jax.experimental import pallas as pl
from jax.experimental.pallas import tpu as pltpu
from jax.sharding import PartitionSpec as P

EMBED_SIZE = 1024
HEAD_SIZE = 64
FF = 4096
LOWRANK_DECAY = 64
LOWRANK_RATE = 64
LOWRANK_VALUE = 32
LOWRANK_GATE = 128
BLOCK = 64
NS_STEPS = 5


HIGHEST = lax.Precision.HIGHEST
COEFF_A = 3.4445
COEFF_B = -4.775
COEFF_C = 2.0315
ORTHO_STEP_RATE = 0.5
VECTOR_RATE = 0.75
DECAY_KEEP = 0.5


def passed_along(value, axis, steps):
    count = lax.axis_size(axis)
    first, last = (max(0, -steps), min(count, count - steps))
    return lax.ppermute(value, axis, [(source, source + steps) for source in range(first, last)])


def layer_norm(content_lines, gain, bias):
    centered = content_lines - jnp.mean(content_lines, axis=-1, keepdims=True)
    variance = jnp.mean(centered * centered, axis=-1, keepdims=True)
    return centered * lax.rsqrt(variance + 1e-05) * gain + bias


def product(left, right):
    return jnp.dot(left, right, preferred_element_type=jnp.float32)


def inner_rows(left, right):
    return jnp.einsum("ta,tb->ab", left, right, preferred_element_type=jnp.float32)


def outer_back(left, right):
    return jnp.einsum("ta,ba->tb", left, right, preferred_element_type=jnp.float32)


def neighbour_row(row, offset):
    return passed_along(row, "seq", offset)


def from_before(row, is_first, stride):
    return jnp.where(is_first, 0.0, neighbour_row(row, stride))


def from_after(row, is_first, stride):
    return neighbour_row(jnp.where(is_first, 0.0, row), -stride)


def head_total(term):
    return lax.psum(term, "head")


def vector_step(param, moved_rows):
    blocks = moved_rows.reshape(
        moved_rows.shape[:-1] + (moved_rows.shape[-1] // HEAD_SIZE, HEAD_SIZE)
    )
    scale = jnp.sqrt(jnp.mean(blocks * blocks, axis=-1, keepdims=True)) + 1e-06
    return param - VECTOR_RATE * (blocks / scale).reshape(moved_rows.shape)


BF = jnp.bfloat16
F32 = jnp.float32
SQUASH = math.exp(-0.5)


def split(x):
    high = x.astype(BF)
    return high, (x - high.astype(F32)).astype(BF)


DIMS = {"nn": ((1,), (0,)), "nt": ((1,), (1,)), "tn": ((0,), (0,))}


def dot_kind(a, b, kind):
    return lax.dot_general(a, b, (DIMS[kind], ((), ())), preferred_element_type=F32)


class Pairing:
    def __init__(self, heads, passes):
        self.heads = heads
        self.passes = passes
        width = heads * HEAD_SIZE
        rows = lax.broadcasted_iota(jnp.int32, (width, width), 0) // HEAD_SIZE
        cols = lax.broadcasted_iota(jnp.int32, (width, width), 1) // HEAD_SIZE
        self.same = rows == cols

    def parts(self, x):
        return split(x) if self.passes == 3 else (x.astype(BF),)

    def spread(self, x):
        zero = jnp.zeros((), BF)
        return tuple(
            jnp.where(self.same, jnp.concatenate([item] * self.heads, axis=0), zero)
            for item in self.parts(x)
        )

    def run(self, left, right, kind):
        total = dot_kind(left[0], right[0], kind)
        if len(left) > 1:
            total = total + (dot_kind(left[0], right[1], kind) + dot_kind(left[1], right[0], kind))
        return total

    def nn(self, a, b_spread):
        return self.run(self.parts(a), b_spread, "nn")

    def nt(self, a, b_spread):
        return self.run(self.parts(a), b_spread, "nt")

    def tn(self, a, b):
        full = jnp.where(self.same, self.run(self.parts(a), self.parts(b), "tn"), 0.0)
        total = full[:HEAD_SIZE]
        for head in range(1, self.heads):
            total = total + full[head * HEAD_SIZE : (head + 1) * HEAD_SIZE]
        return total


def head_sum(x, same):
    ones = same.astype(BF)
    high, low = split(x)
    return dot_kind(high, ones, "nn") + dot_kind(low, ones, "nn")


def exact_left(ones, x):
    high, rest = split(x)
    third = (x - high.astype(F32) - rest.astype(F32)).astype(BF)
    return (
        dot_kind(ones, high, "nn") + dot_kind(ones, rest, "nn") + dot_kind(ones, third, "nn")
    )


def sigmoid(x):
    return 1.0 / (1.0 + jnp.exp(-x))


def side_iotas(width):
    rows = lax.broadcasted_iota(jnp.int32, (HEAD_SIZE, width), 0)
    cols = lax.broadcasted_iota(jnp.int32, (HEAD_SIZE, width), 1) % HEAD_SIZE
    return rows, cols


def prepared(keys, values, up_w, up_a, up_v, first, scale, offset, forget, same):
    sig_w = sigmoid(forget + up_w)
    log_decay = -SQUASH * sig_w
    rate = sigmoid(offset[0:1] + up_a)
    sig_v = sigmoid(offset[1:2] + up_v)
    mixed = values + (first - values) * sig_v
    scaled = keys * scale[0:1]
    inverse = lax.rsqrt(head_sum(scaled * scaled, same) + 1e-05)
    unit = scaled * inverse
    grown = 1.0 + (rate - 1.0) * scale[1:2]
    return sig_w, log_decay, rate, sig_v, mixed, inverse, unit, grown


def decays(log_decay):
    rows = lax.broadcasted_iota(jnp.int32, (BLOCK, BLOCK), 0)
    cols = lax.broadcasted_iota(jnp.int32, (BLOCK, BLOCK), 1)
    total = exact_left((rows >= cols).astype(BF), log_decay)
    last = total[BLOCK - 1 : BLOCK]
    return jnp.exp(total), jnp.exp(total - log_decay), jnp.exp(-total), jnp.exp(last - total), jnp.exp(last)


def forward_local_kernel(
    heads, rec_ref, keys_ref, values_ref, upw_ref, upa_ref, upv_ref, first_ref, scale_ref, offset_ref, forget_ref,
    summary_ref, blocks_ref, read_ref, local_ref, inv_ref, wide_ref, fixed_ref, prb_ref, prk_ref, pak_ref,
):
    width = heads * HEAD_SIZE
    pair = Pairing(heads, 3)
    rows, cols = side_iotas(width)
    strict, upto = rows > cols, rows >= cols
    eye = (rows == cols).astype(F32)
    scale, offset, forget = scale_ref[...], offset_ref[...], forget_ref[...]
    count = rec_ref.shape[0] // BLOCK
    moves = []
    for index in range(count):
        span = slice(index * BLOCK, (index + 1) * BLOCK)
        keys = keys_ref[span]
        sig_w, log_decay, rate, sig_v, mixed, inverse, unit, grown = prepared(
            keys, values_ref[span], upw_ref[span], upa_ref[span], upv_ref[span],
            first_ref[span].astype(F32), scale, offset, forget, pair.same,
        )
        e_total, e_before, e_back, e_tail, e_last = decays(log_decay)
        beta, new_keys = unit * rate, keys * grown
        grown_r, grown_a = rec_ref[span] * e_total, -unit * e_before
        both = jnp.concatenate([grown_a, grown_r], axis=0)
        on_b = pair.nt(both, pair.spread(beta * e_back))
        on_k = pair.nt(both, pair.spread(new_keys * e_back))
        pab = jnp.where(strict, on_b[:BLOCK], 0.0)
        pak = jnp.where(strict, on_k[:BLOCK], 0.0)
        prb = jnp.where(upto, on_b[BLOCK:], 0.0)
        prk = jnp.where(upto, on_k[BLOCK:], 0.0)
        size = 1
        solved = eye
        while size < BLOCK:
            corner = (
                ((rows // size) % 2 == 1) & ((cols // size) % 2 == 0)
                & (rows // (2 * size) == cols // (2 * size))
            )
            piece = jnp.where(corner, pab, 0.0)
            if size > 1:
                piece = pair.nn(pair.nn(solved, pair.spread(piece)), pair.spread(solved))
            solved = solved + piece
            size *= 2
        mixed_spread = pair.spread(mixed)
        on_v = pair.nn(jnp.concatenate([pak, prk], axis=0), mixed_spread)
        wide = pair.nn(solved, pair.spread(grown_a))
        fixed = pair.nn(solved, pair.spread(on_v[:BLOCK]))
        read_ref[span] = grown_r + pair.nn(prb, pair.spread(wide))
        local_ref[span] = on_v[BLOCK:] + pair.nn(prb, pair.spread(fixed))
        tail_b, tail_k = beta * e_tail, new_keys * e_tail
        move = eye * e_last + pair.tn(wide, tail_b)
        add = pair.tn(jnp.concatenate([fixed, mixed], axis=0), jnp.concatenate([tail_b, tail_k], axis=0))
        blocks_ref[index, :BLOCK] = move
        blocks_ref[index, BLOCK:] = add
        inv_ref[span] = solved
        wide_ref[span] = wide
        fixed_ref[span] = fixed
        prb_ref[span] = prb
        prk_ref[span] = prk
        pak_ref[span] = pak
        moves.append((move, add))
    summary = jnp.concatenate(moves[0], axis=0)
    for move, add in moves[1:]:
        summary = pair.nn(summary, pair.spread(move))
        summary = jnp.concatenate([summary[:BLOCK], summary[BLOCK:] + add], axis=0)
    summary_ref[...] = summary


def group_norm(outputs, same):
    mean = head_sum(outputs, same) * (1.0 / HEAD_SIZE)
    centered = outputs - mean
    variance = head_sum(centered * centered, same) * (1.0 / HEAD_SIZE)
    inverse = lax.rsqrt(variance + 0.00064)
    return centered * inverse, inverse


def forward_state_kernel(
    heads, start_ref, others_ref, flags_ref, blocks_ref, read_ref, local_ref, rec_ref, keys_ref, values_ref, upa_ref, upv_ref,
    first_ref, gate_ref, scale_ref, offset_ref, reward_ref, branch_ref, states_ref, outputs_ref,
):
    pair = Pairing(heads, 3)
    count = rec_ref.shape[0] // BLOCK
    state = start_ref[...]
    for index in range(others_ref.shape[0]):
        move = pair.spread(others_ref[index, :BLOCK])
        moved = pair.nn(state, move) + others_ref[index, BLOCK:]
        state = jnp.where(flags_ref[index : index + 1] > 0.0, moved, state)
    scale, offset, reward = scale_ref[...], offset_ref[...], reward_ref[...]
    for index in range(count):
        span = slice(index * BLOCK, (index + 1) * BLOCK)
        states_ref[index] = state
        outputs_ref[span] = pair.nt(read_ref[span], pair.spread(state)) + local_ref[span]
        if index < count - 1:
            state = pair.nn(state, pair.spread(blocks_ref[index, :BLOCK])) + blocks_ref[index, BLOCK:]
    normal, _ = group_norm(outputs_ref[...], pair.same)
    rate = sigmoid(offset[0:1] + upa_ref[...])
    values = values_ref[...]
    mixed = values + (first_ref[...].astype(F32) - values) * sigmoid(offset[1:2] + upv_ref[...])
    new_keys = keys_ref[...] * (1.0 + (rate - 1.0) * scale[1:2])
    bonus = head_sum(rec_ref[...] * new_keys * reward, pair.same)
    branch = (normal * scale[2:3] + offset[2:3] + bonus * mixed) * gate_ref[...]
    branch_ref[...] = branch.astype(BF)


def backward_local_kernel(
    heads, slope_ref, outputs_ref, read_ref, blocks_ref, rec_ref, keys_ref, values_ref, upa_ref, upv_ref, first_ref,
    gate_ref, scale_ref, offset_ref, reward_ref,
    local_ref, steps_ref, slope_out_ref, gate_out_ref, rec_out_ref, keys_out_ref, values_out_ref, sums_ref,
):
    pair = Pairing(heads, 3)
    same = pair.same
    count = rec_ref.shape[0] // BLOCK
    scale, offset, reward = scale_ref[...], offset_ref[...], reward_ref[...]
    normal, inverse = group_norm(outputs_ref[...], same)
    rate = sigmoid(offset[0:1] + upa_ref[...])
    values = values_ref[...]
    mixed = values + (first_ref[...].astype(F32) - values) * sigmoid(offset[1:2] + upv_ref[...])
    new_keys = keys_ref[...] * (1.0 + (rate - 1.0) * scale[1:2])
    rec = rec_ref[...]
    bonus = head_sum(rec * new_keys * reward, same)
    slope = slope_ref[...]
    gate_out_ref[...] = (slope * (normal * scale[2:3] + offset[2:3] + bonus * mixed)).astype(BF)
    inner = slope * gate_ref[...]
    d_bonus = head_sum(inner * mixed, same)
    rec_out_ref[...] = d_bonus * new_keys * reward
    keys_out_ref[...] = d_bonus * rec * reward
    values_out_ref[...] = inner * bonus
    d_normal = inner * scale[2:3]
    mean_a = head_sum(d_normal, same) * (1.0 / HEAD_SIZE)
    mean_b = head_sum(d_normal * normal, same) * (1.0 / HEAD_SIZE)
    slope_out_ref[...] = inverse * (d_normal - mean_a - normal * mean_b)
    sums_ref[0:1] = jnp.sum(inner * normal, axis=0, keepdims=True)
    sums_ref[1:2] = jnp.sum(inner, axis=0, keepdims=True)
    sums_ref[2:3] = jnp.sum(d_bonus * rec * new_keys, axis=0, keepdims=True)
    sums_ref[3:8] = jnp.zeros((5, slope.shape[1]), F32)
    total = None
    for index in range(count - 1, -1, -1):
        span = slice(index * BLOCK, (index + 1) * BLOCK)
        step = pair.tn(slope_out_ref[span], read_ref[span])
        steps_ref[index] = step
        total = step if total is None else pair.nt(total, pair.spread(blocks_ref[index, :BLOCK])) + step
    local_ref[...] = total


def backward_state_kernel(
    heads, moves_ref, locals_ref, flags_ref, states_ref, blocks_ref, steps_ref, inv_ref, wide_ref, fixed_ref, prb_ref, prk_ref,
    pak_ref, slope_ref, rec_extra_ref, keys_extra_ref, values_extra_ref, rec_ref, keys_ref, values_ref, upw_ref, upa_ref, upv_ref,
    first_ref, scale_ref, offset_ref, forget_ref,
    d_state_ref, d_rec_ref, d_keys_ref, d_values_ref, d_upw_ref, d_upa_ref, d_upv_ref, d_first_ref, sums_ref,
):
    pair = Pairing(heads, 3)
    same = pair.same
    width = heads * HEAD_SIZE
    rows, cols = side_iotas(width)
    strict, upto = rows > cols, rows >= cols
    count = rec_ref.shape[0] // BLOCK
    scale, offset, forget = scale_ref[...], offset_ref[...], forget_ref[...]
    outgoing = jnp.zeros((HEAD_SIZE, width), F32)
    for index in range(locals_ref.shape[0] - 1, -1, -1):
        moved = pair.nt(outgoing, pair.spread(moves_ref[index])) + locals_ref[index]
        outgoing = jnp.where(flags_ref[index : index + 1] > 0.0, moved, outgoing)
    row_ids = lax.broadcasted_iota(jnp.int32, (BLOCK, 2 * BLOCK), 0)
    col_ids = lax.broadcasted_iota(jnp.int32, (BLOCK, 2 * BLOCK), 1)
    later = ((col_ids < BLOCK) & (col_ids >= row_ids)) | (col_ids - BLOCK > row_ids)
    later = later.astype(BF)
    sums = [jnp.zeros((1, width), F32) for _ in range(5)]
    for index in range(count - 1, -1, -1):
        span = slice(index * BLOCK, (index + 1) * BLOCK)
        keys, values = keys_ref[span], values_ref[span]
        first = first_ref[span].astype(F32)
        sig_w, log_decay, rate, sig_v, mixed, inverse, unit, grown = prepared(
            keys, values, upw_ref[span], upa_ref[span], upv_ref[span],
            first, scale, offset, forget, same,
        )
        e_total, e_before, e_back, e_tail, e_last = decays(log_decay)
        beta, new_keys = unit * rate, keys * grown
        grown_r, grown_a = rec_ref[span] * e_total, -unit * e_before
        shrunk_b, shrunk_k = beta * e_back, new_keys * e_back
        tail_b, tail_k = beta * e_tail, new_keys * e_tail
        state, slope = states_ref[index], slope_ref[span]
        state_spread, outgoing_spread = pair.spread(state), pair.spread(outgoing)
        carried = pair.nt(wide_ref[span], state_spread) + fixed_ref[span]
        tails = pair.nt(jnp.concatenate([tail_b, tail_k], axis=0), outgoing_spread)
        d_carried = pair.tn(prb_ref[span], slope) + tails[:BLOCK]
        d_right = pair.tn(inv_ref[span], d_carried)
        slopes = jnp.concatenate([d_right, slope], axis=0)
        d_mixed = tails[BLOCK:] + values_extra_ref[span] + pair.tn(
            jnp.concatenate([pak_ref[span], prk_ref[span]], axis=0), slopes
        )
        d_grown = pair.nn(slopes, state_spread)
        on_c = pair.nt(slopes, pair.spread(carried))
        on_v = pair.nt(slopes, pair.spread(mixed))
        d_b = jnp.concatenate([jnp.where(strict, on_c[:BLOCK], 0.0), jnp.where(upto, on_c[BLOCK:], 0.0)], axis=0)
        d_k = jnp.concatenate([jnp.where(strict, on_v[:BLOCK], 0.0), jnp.where(upto, on_v[BLOCK:], 0.0)], axis=0)
        d_grown = d_grown + pair.nn(d_b, pair.spread(shrunk_b)) + pair.nn(d_k, pair.spread(shrunk_k))
        both = jnp.concatenate([grown_a, grown_r], axis=0)
        d_shrunk_b, d_shrunk_k = pair.tn(d_b, both), pair.tn(d_k, both)
        d_tails = pair.nn(jnp.concatenate([carried, mixed], axis=0), outgoing_spread)
        d_tail_b, d_tail_k = d_tails[:BLOCK], d_tails[BLOCK:]
        d_last = jnp.sum(state * outgoing, axis=0, keepdims=True) * e_last + jnp.sum(
            d_tail_b * tail_b + d_tail_k * tail_k, axis=0, keepdims=True
        )
        d_grown_a, d_grown_r = d_grown[:BLOCK], d_grown[BLOCK:]
        d_total = (
            d_grown_r * grown_r - d_shrunk_b * shrunk_b - d_shrunk_k * shrunk_k
            - d_tail_b * tail_b - d_tail_k * tail_k
        )
        d_log = exact_left(later, jnp.concatenate([d_total, d_grown_a * grown_a], axis=0)) + d_last
        d_rec_ref[span] = (d_grown_r * e_total + rec_extra_ref[span]).astype(BF)
        d_alpha = d_grown_a * e_before
        d_beta = d_shrunk_b * e_back + d_tail_b * e_tail
        d_new = d_shrunk_k * e_back + d_tail_k * e_tail + keys_extra_ref[span]
        d_unit = d_beta * rate - d_alpha
        d_rate = d_beta * unit + d_new * keys * scale[1:2]
        d_scaled = inverse * (d_unit - unit * head_sum(d_unit * unit, same))
        d_keys_ref[span] = (d_new * grown + d_scaled * scale[0:1]).astype(BF)
        d_upw = d_log * log_decay * (1.0 - sig_w)
        d_upa = d_rate * rate * (1.0 - rate)
        d_upv = d_mixed * (first - values) * sig_v * (1.0 - sig_v)
        d_upw_ref[span] = d_upw.astype(BF)
        d_upa_ref[span] = d_upa.astype(BF)
        d_upv_ref[span] = d_upv.astype(BF)
        d_values_ref[span] = (d_mixed * (1.0 - sig_v)).astype(BF)
        d_first_ref[span] = d_mixed * sig_v
        terms = (d_scaled * keys, d_new * keys * (rate - 1.0), d_upa, d_upv, d_upw)
        sums = [total + jnp.sum(term, axis=0, keepdims=True) for total, term in zip(sums, terms)]
        outgoing = pair.nt(outgoing, pair.spread(blocks_ref[index, :BLOCK])) + steps_ref[index]
    d_state_ref[...] = outgoing
    for index in range(5):
        sums_ref[index : index + 1] = sums[index]
    sums_ref[5:8] = jnp.zeros((3, width), F32)


def local_call(body, heads, results, operands):
    return pl.pallas_call(
        functools.partial(body, heads),
        out_shape=tuple(jax.ShapeDtypeStruct(shape, dtype) for shape, dtype in results),
        in_specs=[pl.BlockSpec(memory_space=pltpu.VMEM)] * len(operands),
        out_specs=tuple(pl.BlockSpec(memory_space=pltpu.VMEM) for _ in results),
        compiler_params=pltpu.CompilerParams(vmem_limit_bytes=48 * 1024 * 1024),
    )(*operands)


def cheap(left, right):
    return jnp.dot(left.astype(BF), right.astype(BF), preferred_element_type=F32)


def close(left, right):
    return jnp.dot(left, right, precision=lax.Precision.HIGH, preferred_element_type=F32)


def exact(left, right):
    return jnp.matmul(left, right, precision=HIGHEST, preferred_element_type=F32)


def shifted_terms(gram, shift, dot):
    rest = gram - shift * jnp.eye(gram.shape[-1], dtype=F32)
    value = COEFF_A + COEFF_B * shift + COEFF_C * shift * shift
    return value, (COEFF_B + 2.0 * COEFF_C * shift) * rest + COEFF_C * dot(rest, rest), rest


def newton_whole(current):
    for step in range(NS_STEPS):
        dot = cheap if step < 3 else close
        gram = dot(current, current.T)
        shift = jnp.trace(gram) / gram.shape[0]
        value, terms, _ = shifted_terms(gram, shift, dot)
        current = value * current + dot(terms, current)
    return current


def gram_next(gram, shift, value, terms, rest, dot):
    square = 2.0 * value * terms + dot(terms, terms)
    return value * value * gram + shift * square + dot(rest, square)


def newton_grams(current, gram, shift_of, dots, applies):
    for step in range(NS_STEPS):
        shift = shift_of(gram)
        value, terms, rest = shifted_terms(gram, shift, dots[step])
        current = value * current + applies[step](terms, current)
        if step < NS_STEPS - 1:
            gram = gram_next(gram, shift, value, terms, rest, dots[step])
    return current


def on_device(
    input_embeddings,
    loss_adjoint,
    earliest_tier_content,
    opening_memory,
    live_extents,
    lagged_blend_coeffs,
    standardize_scales,
    standardize_offsets,
    adapter_narrowing_coeffs,
    adapter_widening_coeffs,
    attention_scale_lines,
    attention_offset_lines,
    present_reward_array,
    forgetting_offset,
    readin_maps,
    emission_coeffs,
    feedforward_address_coeffs,
    feedforward_content_coeffs,
    lagged_blend_velocity,
    standardize_scale_velocity,
    standardize_offset_velocity,
    narrowing_velocity,
    widening_velocity,
    attention_scale_velocity,
    attention_offset_velocity,
    reward_velocity_array,
    forgetting_velocity,
    readin_velocity,
    emission_velocity,
    feedforward_address_velocity,
    feedforward_content_velocity,
):
    seq_count = lax.axis_size("seq")
    seq_index = lax.axis_index("seq")
    overall_tally = input_embeddings.shape[0]
    stride = live_extents.shape[0]
    per_sequence = seq_count // stride
    place = seq_index // stride
    sequence_id = seq_index % stride
    is_first = place == 0
    is_last = place == per_sequence - 1
    slot_ids = place * overall_tally + lax.iota(jnp.int32, overall_tally)
    live = (slot_ids < live_extents[sequence_id]).astype(jnp.float32)[:, None]
    sequence_edges = (
        0,
        LOWRANK_DECAY,
        LOWRANK_DECAY + LOWRANK_RATE,
        LOWRANK_DECAY + LOWRANK_RATE + LOWRANK_VALUE,
        LOWRANK_DECAY + LOWRANK_RATE + LOWRANK_VALUE + LOWRANK_GATE,
    )
    sequence_spans = list(zip(sequence_edges[:-1], sequence_edges[1:]))
    sources = (1, 4, 3, 5)
    inputs = input_embeddings.astype(jnp.float32)
    normed, first_pull = jax.vjp(layer_norm, inputs, standardize_scales[0], standardize_offsets[0])
    before = jnp.concatenate([from_before(normed[-1:], is_first, stride), normed[:-1]], axis=0)
    delta = before - normed
    mixes = [
        (normed + delta * lagged_blend_coeffs[index]).astype(jnp.bfloat16) for index in range(6)
    ]
    weights = readin_maps.astype(jnp.bfloat16)
    down_matrix = adapter_narrowing_coeffs.astype(jnp.bfloat16)
    up_matrix = adapter_widening_coeffs.astype(jnp.bfloat16)
    acceptance_lines = product(mixes[0], weights[0])
    address_lines = product(mixes[2], weights[1])
    content_lines = product(mixes[3], weights[2])
    hidden = [
        product(
            mixes[sources[index]],
            down_matrix[:, sequence_spans[index][0] : sequence_spans[index][1]],
        )
        for index in range(4)
    ]
    tanh_w = jnp.tanh(hidden[0])
    gate_sig = jax.nn.sigmoid(hidden[3])
    acts = [
        tanh_w.astype(jnp.bfloat16),
        hidden[1].astype(jnp.bfloat16),
        hidden[2].astype(jnp.bfloat16),
        gate_sig.astype(jnp.bfloat16),
    ]
    widened_lines = [
        product(acts[index], up_matrix[sequence_spans[index][0] : sequence_spans[index][1]])
        for index in range(4)
    ]
    width = acceptance_lines.shape[1]
    local_heads = width // HEAD_SIZE
    blocks_count = overall_tally // BLOCK
    lines = ((overall_tally, width), F32)
    low_lines = ((overall_tally, width), BF)
    tiny = ((8, width), F32)
    state_shape = ((HEAD_SIZE, width), F32)
    steps_shape = ((blocks_count, HEAD_SIZE, width), F32)
    pieces_shape = ((blocks_count, 2 * HEAD_SIZE, width), F32)
    reward_row = present_reward_array.reshape(1, width)
    forget_row = forgetting_offset.reshape(1, width)
    raw_lines = (address_lines, content_lines)
    summary, pieces, read, local, solved, wide, fixed, pair_rb, pair_rk, pair_ak = local_call(
        forward_local_kernel,
        local_heads,
        [((2 * HEAD_SIZE, width), F32), pieces_shape] + [lines] * 8,
        (acceptance_lines, *raw_lines, *widened_lines[:3], earliest_tier_content)
        + (attention_scale_lines, attention_offset_lines, forget_row),
    )
    distances = range(1, per_sequence)
    earlier = jnp.stack([passed_along(summary, "seq", far * stride) for far in distances][::-1])
    later_moves = jnp.stack(
        [passed_along(summary[:HEAD_SIZE], "seq", -far * stride) for far in distances]
    )
    earlier_flags = jnp.stack([(place >= far).astype(F32) for far in distances][::-1])
    later_flags = jnp.stack([(place + far < per_sequence).astype(F32) for far in distances])
    earlier_flags = jnp.broadcast_to(earlier_flags[:, None], (per_sequence - 1, width))
    later_flags = jnp.broadcast_to(later_flags[:, None], (per_sequence - 1, width))
    own_start = lax.dynamic_index_in_dim(opening_memory, sequence_id, 0, keepdims=False)
    own_start = jnp.swapaxes(own_start, 0, 1).reshape(HEAD_SIZE, width)
    adapter_result, states, outputs = local_call(
        forward_state_kernel,
        local_heads,
        [low_lines, steps_shape, lines],
        (own_start, earlier, earlier_flags, pieces, read, local, acceptance_lines, *raw_lines)
        + (widened_lines[1], widened_lines[2], earliest_tier_content, widened_lines[3])
        + (attention_scale_lines, attention_offset_lines, reward_row),
    )
    out_low = emission_coeffs.astype(jnp.bfloat16)
    attended = inputs + head_total(product(adapter_result, out_low))
    normed_two, second_pull = jax.vjp(
        layer_norm, attended, standardize_scales[1], standardize_offsets[1]
    )
    before_two = jnp.concatenate(
        [from_before(normed_two[-1:], is_first, stride), normed_two[:-1]], axis=0
    )
    delta_two = before_two - normed_two
    key_in = (normed_two + delta_two * lagged_blend_coeffs[6]).astype(jnp.bfloat16)
    keys_low = feedforward_address_coeffs.astype(jnp.bfloat16)
    values_low = feedforward_content_coeffs.astype(jnp.bfloat16)
    hidden_ffn = product(key_in, keys_low)
    activated = jnp.square(jax.nn.relu(hidden_ffn)).astype(jnp.bfloat16)
    result = attended + head_total(product(activated, values_low))
    block_output = (result * live).astype(jnp.bfloat16)
    grad_result = loss_adjoint.astype(jnp.float32) * live
    grad_low = grad_result.astype(jnp.bfloat16)
    grad_ffnvalue = inner_rows(activated, grad_low)
    grad_hidden = (outer_back(grad_low, values_low) * 2.0 * jax.nn.relu(hidden_ffn)).astype(
        jnp.bfloat16
    )
    grad_ffnkey = inner_rows(key_in, grad_hidden)
    grad_ffnkey, grad_ffnvalue = lax.psum((grad_ffnkey, grad_ffnvalue), "seq")
    grad_keyin = lax.psum(outer_back(grad_hidden, keys_low), "head")
    carry_two = grad_keyin * lagged_blend_coeffs[6]
    grad_normed_two = (
        grad_keyin
        - carry_two
        + jnp.concatenate([carry_two[1:], from_after(carry_two[:1], is_first, stride)], axis=0)
    )
    grad_attended, grad_gain_two, grad_bias_two = second_pull(grad_normed_two)
    grad_attended = grad_attended + grad_result
    grad_attended_low = grad_attended.astype(jnp.bfloat16)
    grad_output = inner_rows(adapter_result, grad_attended_low)
    grad_branch = outer_back(grad_attended_low, out_low)
    (
        state_local,
        steps,
        slope,
        grad_gate,
        acceptance_extra,
        address_extra,
        content_extra,
        sums_a,
    ) = local_call(
        backward_local_kernel,
        local_heads,
        [state_shape, steps_shape, lines, low_lines, lines, lines, lines, tiny],
        (grad_branch, outputs, read, pieces, acceptance_lines, *raw_lines)
        + (widened_lines[1], widened_lines[2], earliest_tier_content, widened_lines[3])
        + (attention_scale_lines, attention_offset_lines, reward_row),
    )
    later_locals = jnp.stack([passed_along(state_local, "seq", -far * stride) for far in distances])
    (
        grad_state_in,
        grad_rec_low,
        grad_key_low,
        grad_value_low,
        grad_up_w,
        grad_up_a,
        grad_up_v,
        grad_first,
        sums_b,
    ) = local_call(
        backward_state_kernel,
        local_heads,
        [state_shape] + [low_lines] * 6 + [lines, tiny],
        (later_moves, later_locals, later_flags, states, pieces, steps, solved, wide, fixed)
        + (pair_rb, pair_rk, pair_ak, slope, acceptance_extra, address_extra, content_extra)
        + (acceptance_lines, *raw_lines, *widened_lines[:3], earliest_tier_content)
        + (attention_scale_lines, attention_offset_lines, forget_row),
    )
    grad_state_in = jnp.swapaxes(grad_state_in.reshape(HEAD_SIZE, local_heads, HEAD_SIZE), 0, 1)
    grad_headgain = jnp.concatenate([sums_b[0:2], sums_a[0:1]], axis=0)
    grad_headbias = jnp.concatenate([sums_b[2:4], sums_a[1:2]], axis=0)
    reward_loss_slope = sums_a[2]
    grad_decay = sums_b[4]
    grad_lift_low = [grad_up_w, grad_up_a, grad_up_v, grad_gate]
    grad_project = jnp.stack(
        [
            inner_rows(mixes[0], grad_rec_low),
            inner_rows(mixes[2], grad_key_low),
            inner_rows(mixes[3], grad_value_low),
        ]
    )
    grad_up = jnp.concatenate(
        [inner_rows(acts[index], grad_lift_low[index]) for index in range(4)], axis=0
    )
    split_grads = (
        outer_back(grad_rec_low, weights[0]),
        outer_back(grad_key_low, weights[1]),
        outer_back(grad_value_low, weights[2]),
    )
    split_ids = (0, 2, 3)
    norm_part = sum(
        (split_grads[index] * (1.0 - lagged_blend_coeffs[split_ids[index]]) for index in range(3))
    )
    prev_part = sum(
        (split_grads[index] * lagged_blend_coeffs[split_ids[index]] for index in range(3))
    )
    shift_part = jnp.stack([jnp.sum(item * delta, axis=0) for item in split_grads])
    acts_part = jnp.concatenate(
        [
            outer_back(
                grad_lift_low[index], up_matrix[sequence_spans[index][0] : sequence_spans[index][1]]
            )
            for index in range(4)
        ],
        axis=1,
    )
    acts_sum, shift_sum = lax.psum((acts_part, shift_part), "head")
    normed_part = norm_part + jnp.concatenate(
        [prev_part[1:], from_after(prev_part[:1], is_first, stride)], axis=0
    )
    norm_sum = lax.psum(normed_part, "head")
    act_grads = [acts_sum[:, start_index:stop_index] for start_index, stop_index in sequence_spans]
    grad_hidden_low = [
        (act_grads[0] * (1.0 - tanh_w * tanh_w)).astype(jnp.bfloat16),
        act_grads[1].astype(jnp.bfloat16),
        act_grads[2].astype(jnp.bfloat16),
        (act_grads[3] * gate_sig * (1.0 - gate_sig)).astype(jnp.bfloat16),
    ]
    grad_down = jnp.concatenate(
        [inner_rows(mixes[sources[index]], grad_hidden_low[index]) for index in range(4)], axis=1
    )
    rep_grads = [
        outer_back(
            grad_hidden_low[index],
            down_matrix[:, sequence_spans[index][0] : sequence_spans[index][1]],
        )
        for index in range(4)
    ]
    grad_normed = norm_sum + sum(
        (rep_grads[index] * (1.0 - lagged_blend_coeffs[sources[index]]) for index in range(4))
    )
    grad_prev = sum(
        (rep_grads[index] * lagged_blend_coeffs[sources[index]] for index in range(4))
    )
    grad_normed = grad_normed + jnp.concatenate(
        [grad_prev[1:], from_after(grad_prev[:1], is_first, stride)], axis=0
    )
    grad_inputs, grad_gain_one, grad_bias_one = first_pull(grad_normed)
    tokens_grad = grad_attended + grad_inputs
    rep_shift = [jnp.sum(item * delta, axis=0) for item in rep_grads]
    grad_shift = jnp.stack(
        [
            shift_sum[0],
            rep_shift[0],
            shift_sum[1],
            shift_sum[2] + rep_shift[2],
            rep_shift[1],
            rep_shift[3],
            jnp.sum(grad_keyin * delta_two, axis=0),
        ]
    )
    choose = ((lax.iota(jnp.int32, stride) == sequence_id) & is_first).astype(jnp.float32)
    state_part = choose[:, None, None, None] * grad_state_in[None]
    summed = lax.psum(
        (
            grad_shift,
            jnp.stack([grad_gain_one, grad_gain_two]),
            jnp.stack([grad_bias_one, grad_bias_two]),
            grad_down,
            grad_up,
            grad_headgain,
            grad_headbias,
            reward_loss_slope,
            grad_decay,
            grad_project,
            grad_output,
            state_part,
        ),
        "seq",
    )
    summed = (*summed[:11], grad_ffnkey, grad_ffnvalue, summed[11])
    learnable_tensors = (
        lagged_blend_coeffs,
        standardize_scales,
        standardize_offsets,
        adapter_narrowing_coeffs,
        adapter_widening_coeffs,
        attention_scale_lines,
        attention_offset_lines,
        present_reward_array,
        forgetting_offset,
        readin_maps,
        emission_coeffs,
        feedforward_address_coeffs,
        feedforward_content_coeffs,
    )
    velocity_collection = (
        lagged_blend_velocity,
        standardize_scale_velocity,
        standardize_offset_velocity,
        narrowing_velocity,
        widening_velocity,
        attention_scale_velocity,
        attention_offset_velocity,
        reward_velocity_array,
        forgetting_velocity,
        readin_velocity,
        emission_velocity,
        feedforward_address_velocity,
        feedforward_content_velocity,
    )
    moved_rows = [
        DECAY_KEEP * velocity + grad for velocity, grad in zip(velocity_collection, summed[:13])
    ]
    next_values = list(learnable_tensors)
    for index in (0, 1, 2, 5, 6, 7, 8):
        next_values[index] = vector_step(learnable_tensors[index], moved_rows[index])
    square_stack = jnp.stack(
        [moved_rows[9][0], moved_rows[9][1], moved_rows[9][2], moved_rows[10].T]
    )
    wide_stack = jnp.stack([moved_rows[11], moved_rows[12].T])
    own_square = lax.dynamic_index_in_dim(square_stack, seq_index % 4, 0, keepdims=False)
    own_wide = lax.dynamic_index_in_dim(wide_stack, seq_index % 2, 0, keepdims=False)
    lift_moved = moved_rows[4]
    sink_moved = moved_rows[3].T
    total_rank = lift_moved.shape[0]
    wide_gram, lift_gram = lax.psum(
        (close(own_wide, own_wide.T), exact(lift_moved, lift_moved.T)), "head"
    )
    whole_square = lax.all_gather(own_square, "head", axis=1, tiled=True)
    square_scale = 1.0 / (jnp.sqrt(jnp.sum(whole_square * whole_square)) + 1e-07)
    whole_square = newton_whole(whole_square * square_scale)
    wide_scale = 1.0 / (jnp.sqrt(jnp.trace(wide_gram)) + 1e-07)
    wide_done = newton_grams(
        own_wide * wide_scale,
        wide_gram * (wide_scale * wide_scale),
        lambda gram: jnp.trace(gram) / gram.shape[0],
        (cheap, cheap, close, close, close),
        (cheap, cheap, cheap, close, close),
    )
    group = jnp.stack(
        [(lax.iota(jnp.int32, total_rank) >= edge).astype(jnp.int32) for edge in sequence_edges[1:4]]
    ).sum(axis=0)
    member = (group[:, None] == group[None, :]).astype(F32)
    sizes = jnp.sum(member, axis=1)
    grams = jnp.stack([lift_gram, exact(sink_moved, sink_moved.T)]) * member
    eye = jnp.eye(total_rank, dtype=F32)
    diagonals = jnp.sum(grams * eye, axis=2)
    scales = 1.0 / (jnp.sqrt(exact(diagonals, member)) + 1e-07)
    grams = grams * (scales * scales)[:, :, None]
    shift_of = lambda gram: (exact(jnp.sum(gram * eye, axis=2), member) / sizes)[:, :, None]
    maps = newton_grams(jnp.broadcast_to(eye, grams.shape), grams, shift_of, [exact] * 5, [exact] * 5)
    maps = maps * scales[:, :, None]
    lift_done = exact(maps[0], lift_moved)
    sink_done = exact(maps[1], sink_moved)
    head_index = lax.axis_index("head")
    square_width = own_square.shape[1]
    square_done = lax.dynamic_slice_in_dim(whole_square, head_index * square_width, square_width, 1)
    share = EMBED_SIZE // seq_count
    start_row = seq_index * share

    def shared_rows(done):
        return lax.all_to_all(
            done.reshape(seq_count, share, done.shape[1]), "seq", 0, 0, tiled=True
        )

    square_rows = shared_rows(square_done)
    wide_rows = shared_rows(wide_done)
    rows_of = lambda item, axis: lax.dynamic_slice_in_dim(item, start_row, share, axis)
    next_values[9] = rows_of(readin_maps, 1) - ORTHO_STEP_RATE * square_rows[:3]
    next_values[10] = rows_of(emission_coeffs, 1) - ORTHO_STEP_RATE * square_rows[3].T
    next_values[11] = rows_of(feedforward_address_coeffs, 0) - ORTHO_STEP_RATE * wide_rows[0]
    next_values[12] = (
        rows_of(feedforward_content_coeffs, 1)
        - ORTHO_STEP_RATE * math.sqrt(max(1.0, FF / EMBED_SIZE)) * wide_rows[1].T
    )
    next_values[4] = adapter_widening_coeffs - ORTHO_STEP_RATE * lift_done
    next_values[3] = adapter_narrowing_coeffs - ORTHO_STEP_RATE * jnp.concatenate(
        [
            math.sqrt(max(1.0, EMBED_SIZE / (stop_index - start_index)))
            * sink_done[start_index:stop_index].T
            for start_index, stop_index in sequence_spans
        ],
        axis=1,
    )
    return (
        block_output,
        tokens_grad,
        grad_first,
        summed[13],
        next_values[0],
        next_values[1],
        next_values[2],
        next_values[3],
        next_values[4],
        next_values[5],
        next_values[6],
        next_values[7],
        next_values[8],
        next_values[9],
        next_values[10],
        next_values[11],
        next_values[12],
        moved_rows[0],
        moved_rows[1],
        moved_rows[2],
        moved_rows[3],
        moved_rows[4],
        moved_rows[5],
        moved_rows[6],
        moved_rows[7],
        moved_rows[8],
        moved_rows[9],
        moved_rows[10],
        moved_rows[11],
        moved_rows[12],
    )


def solution(mesh):
    return jax.shard_map(
        on_device,
        mesh=mesh,
        in_specs=(
            P("seq", None),
            P("seq", None),
            P("seq", "head"),
            P(None, "head", None, None),
            P(),
            P(),
            P(),
            P(),
            P(),
            P(None, "head"),
            P(None, "head"),
            P(None, "head"),
            P("head"),
            P("head"),
            P(None, None, "head"),
            P("head", None),
            P(None, "head"),
            P("head", None),
            P(),
            P(),
            P(),
            P(),
            P(None, "head"),
            P(None, "head"),
            P(None, "head"),
            P("head"),
            P("head"),
            P(None, None, "head"),
            P("head", None),
            P(None, "head"),
            P("head", None),
        ),
        out_specs=(
            P("seq", None),
            P("seq", None),
            P("seq", "head"),
            P(None, "head", None, None),
            P(),
            P(),
            P(),
            P(),
            P(None, "head"),
            P(None, "head"),
            P(None, "head"),
            P("head"),
            P("head"),
            P(None, "seq", "head"),
            P("head", "seq"),
            P("seq", "head"),
            P("head", "seq"),
            P(),
            P(),
            P(),
            P(),
            P(None, "head"),
            P(None, "head"),
            P(None, "head"),
            P("head"),
            P("head"),
            P(None, None, "head"),
            P("head", None),
            P(None, "head"),
            P("head", None),
        ),
        check_vma=False,
    )
```

```python
import functools
import math

import jax
import jax.numpy as jnp
from jax import lax
from jax.experimental import pallas as pl
from jax.experimental.pallas import tpu as pltpu
from jax.sharding import PartitionSpec as P

EMBED_SIZE = 1024
HEAD_SIZE = 64
FF = 4096
LOWRANK_DECAY = 64
LOWRANK_RATE = 64
LOWRANK_VALUE = 32
LOWRANK_GATE = 128
BLOCK = 64
NS_STEPS = 5


HIGHEST = lax.Precision.HIGHEST
COEFF_A = 3.4445
COEFF_B = -4.775
COEFF_C = 2.0315
ORTHO_STEP_RATE = 0.5
VECTOR_RATE = 0.75
DECAY_KEEP = 0.5


def passed_along(value, axis, steps):
    count = lax.axis_size(axis)
    first, last = (max(0, -steps), min(count, count - steps))
    return lax.ppermute(value, axis, [(source, source + steps) for source in range(first, last)])


def layer_norm(content_lines, gain, bias):
    centered = content_lines - jnp.mean(content_lines, axis=-1, keepdims=True)
    variance = jnp.mean(centered * centered, axis=-1, keepdims=True)
    return centered * lax.rsqrt(variance + 1e-05) * gain + bias


def product(left, right):
    return jnp.dot(left, right, preferred_element_type=jnp.float32)


def inner_rows(left, right):
    return jnp.einsum("ta,tb->ab", left, right, preferred_element_type=jnp.float32)


def outer_back(left, right):
    return jnp.einsum("ta,ba->tb", left, right, preferred_element_type=jnp.float32)


def neighbour_row(row, offset):
    return passed_along(row, "seq", offset)


def from_before(row, is_first, stride):
    return jnp.where(is_first, 0.0, neighbour_row(row, stride))


def from_after(row, is_first, stride):
    return neighbour_row(jnp.where(is_first, 0.0, row), -stride)


def head_total(term):
    return lax.psum(term, "head")


def vector_step(param, moved_rows):
    blocks = moved_rows.reshape(
        moved_rows.shape[:-1] + (moved_rows.shape[-1] // HEAD_SIZE, HEAD_SIZE)
    )
    scale = jnp.sqrt(jnp.mean(blocks * blocks, axis=-1, keepdims=True)) + 1e-06
    return param - VECTOR_RATE * (blocks / scale).reshape(moved_rows.shape)


BF = jnp.bfloat16
F32 = jnp.float32
SQUASH = math.exp(-0.5)


def split(x):
    high = x.astype(BF)
    return high, (x - high.astype(F32)).astype(BF)


DIMS = {"nn": ((1,), (0,)), "nt": ((1,), (1,)), "tn": ((0,), (0,))}


def dot_kind(a, b, kind):
    return lax.dot_general(a, b, (DIMS[kind], ((), ())), preferred_element_type=F32)


class Pairing:
    def __init__(self, heads, passes):
        self.heads = heads
        self.passes = passes
        width = heads * HEAD_SIZE
        rows = lax.broadcasted_iota(jnp.int32, (width, width), 0) // HEAD_SIZE
        cols = lax.broadcasted_iota(jnp.int32, (width, width), 1) // HEAD_SIZE
        self.same = rows == cols

    def parts(self, x):
        return split(x) if self.passes == 3 else (x.astype(BF),)

    def spread(self, x):
        zero = jnp.zeros((), BF)
        return tuple(
            jnp.where(self.same, jnp.concatenate([item] * self.heads, axis=0), zero)
            for item in self.parts(x)
        )

    def run(self, left, right, kind):
        total = dot_kind(left[0], right[0], kind)
        if len(left) > 1:
            total = total + (dot_kind(left[0], right[1], kind) + dot_kind(left[1], right[0], kind))
        return total

    def nn(self, a, b_spread):
        return self.run(self.parts(a), b_spread, "nn")

    def nt(self, a, b_spread):
        return self.run(self.parts(a), b_spread, "nt")

    def tn(self, a, b):
        full = jnp.where(self.same, self.run(self.parts(a), self.parts(b), "tn"), 0.0)
        total = full[:HEAD_SIZE]
        for head in range(1, self.heads):
            total = total + full[head * HEAD_SIZE : (head + 1) * HEAD_SIZE]
        return total


def head_sum(x, same):
    ones = same.astype(BF)
    high, low = split(x)
    return dot_kind(high, ones, "nn") + dot_kind(low, ones, "nn")


def exact_left(ones, x):
    high, rest = split(x)
    third = (x - high.astype(F32) - rest.astype(F32)).astype(BF)
    return (
        dot_kind(ones, high, "nn") + dot_kind(ones, rest, "nn") + dot_kind(ones, third, "nn")
    )


def sigmoid(x):
    return 1.0 / (1.0 + jnp.exp(-x))


def side_iotas(width):
    rows = lax.broadcasted_iota(jnp.int32, (HEAD_SIZE, width), 0)
    cols = lax.broadcasted_iota(jnp.int32, (HEAD_SIZE, width), 1) % HEAD_SIZE
    return rows, cols


def prepared(keys, values, up_w, up_a, up_v, first, scale, offset, forget, same):
    sig_w = sigmoid(forget + up_w)
    log_decay = -SQUASH * sig_w
    rate = sigmoid(offset[0:1] + up_a)
    sig_v = sigmoid(offset[1:2] + up_v)
    mixed = values + (first - values) * sig_v
    scaled = keys * scale[0:1]
    inverse = lax.rsqrt(head_sum(scaled * scaled, same) + 1e-05)
    unit = scaled * inverse
    grown = 1.0 + (rate - 1.0) * scale[1:2]
    return sig_w, log_decay, rate, sig_v, mixed, inverse, unit, grown


def decays(log_decay):
    rows = lax.broadcasted_iota(jnp.int32, (BLOCK, BLOCK), 0)
    cols = lax.broadcasted_iota(jnp.int32, (BLOCK, BLOCK), 1)
    total = exact_left((rows >= cols).astype(BF), log_decay)
    last = total[BLOCK - 1 : BLOCK]
    return jnp.exp(total), jnp.exp(total - log_decay), jnp.exp(-total), jnp.exp(last - total), jnp.exp(last)


def forward_local_kernel(
    heads, rec_ref, keys_ref, values_ref, upw_ref, upa_ref, upv_ref, first_ref, scale_ref, offset_ref, forget_ref,
    summary_ref, blocks_ref, read_ref, local_ref, inv_ref, wide_ref, fixed_ref, prb_ref, prk_ref, pak_ref,
):
    width = heads * HEAD_SIZE
    pair = Pairing(heads, 3)
    rows, cols = side_iotas(width)
    strict, upto = rows > cols, rows >= cols
    eye = (rows == cols).astype(F32)
    scale, offset, forget = scale_ref[...], offset_ref[...], forget_ref[...]
    count = rec_ref.shape[0] // BLOCK
    moves = []
    for index in range(count):
        span = slice(index * BLOCK, (index + 1) * BLOCK)
        keys = keys_ref[span]
        sig_w, log_decay, rate, sig_v, mixed, inverse, unit, grown = prepared(
            keys, values_ref[span], upw_ref[span], upa_ref[span], upv_ref[span],
            first_ref[span].astype(F32), scale, offset, forget, pair.same,
        )
        e_total, e_before, e_back, e_tail, e_last = decays(log_decay)
        beta, new_keys = unit * rate, keys * grown
        grown_r, grown_a = rec_ref[span] * e_total, -unit * e_before
        both = jnp.concatenate([grown_a, grown_r], axis=0)
        on_b = pair.nt(both, pair.spread(beta * e_back))
        on_k = pair.nt(both, pair.spread(new_keys * e_back))
        pab = jnp.where(strict, on_b[:BLOCK], 0.0)
        pak = jnp.where(strict, on_k[:BLOCK], 0.0)
        prb = jnp.where(upto, on_b[BLOCK:], 0.0)
        prk = jnp.where(upto, on_k[BLOCK:], 0.0)
        size = 1
        solved = eye
        while size < BLOCK:
            corner = (
                ((rows // size) % 2 == 1) & ((cols // size) % 2 == 0)
                & (rows // (2 * size) == cols // (2 * size))
            )
            piece = jnp.where(corner, pab, 0.0)
            if size > 1:
                piece = pair.nn(pair.nn(solved, pair.spread(piece)), pair.spread(solved))
            solved = solved + piece
            size *= 2
        mixed_spread = pair.spread(mixed)
        on_v = pair.nn(jnp.concatenate([pak, prk], axis=0), mixed_spread)
        wide = pair.nn(solved, pair.spread(grown_a))
        fixed = pair.nn(solved, pair.spread(on_v[:BLOCK]))
        read_ref[span] = grown_r + pair.nn(prb, pair.spread(wide))
        local_ref[span] = on_v[BLOCK:] + pair.nn(prb, pair.spread(fixed))
        tail_b, tail_k = beta * e_tail, new_keys * e_tail
        move = eye * e_last + pair.tn(wide, tail_b)
        add = pair.tn(jnp.concatenate([fixed, mixed], axis=0), jnp.concatenate([tail_b, tail_k], axis=0))
        blocks_ref[index, :BLOCK] = move
        blocks_ref[index, BLOCK:] = add
        inv_ref[span] = solved
        wide_ref[span] = wide
        fixed_ref[span] = fixed
        prb_ref[span] = prb
        prk_ref[span] = prk
        pak_ref[span] = pak
        moves.append((move, add))
    summary = jnp.concatenate(moves[0], axis=0)
    for move, add in moves[1:]:
        summary = pair.nn(summary, pair.spread(move))
        summary = jnp.concatenate([summary[:BLOCK], summary[BLOCK:] + add], axis=0)
    summary_ref[...] = summary


def group_norm(outputs, same):
    mean = head_sum(outputs, same) * (1.0 / HEAD_SIZE)
    centered = outputs - mean
    variance = head_sum(centered * centered, same) * (1.0 / HEAD_SIZE)
    inverse = lax.rsqrt(variance + 0.00064)
    return centered * inverse, inverse


def forward_state_kernel(
    heads, start_ref, others_ref, flags_ref, blocks_ref, read_ref, local_ref, rec_ref, keys_ref, values_ref, upa_ref, upv_ref,
    first_ref, gate_ref, scale_ref, offset_ref, reward_ref, branch_ref, states_ref, outputs_ref,
):
    pair = Pairing(heads, 3)
    count = rec_ref.shape[0] // BLOCK
    state = start_ref[...]
    for index in range(others_ref.shape[0]):
        move = pair.spread(others_ref[index, :BLOCK])
        moved = pair.nn(state, move) + others_ref[index, BLOCK:]
        state = jnp.where(flags_ref[index : index + 1] > 0.0, moved, state)
    scale, offset, reward = scale_ref[...], offset_ref[...], reward_ref[...]
    for index in range(count):
        span = slice(index * BLOCK, (index + 1) * BLOCK)
        states_ref[index] = state
        outputs_ref[span] = pair.nt(read_ref[span], pair.spread(state)) + local_ref[span]
        if index < count - 1:
            state = pair.nn(state, pair.spread(blocks_ref[index, :BLOCK])) + blocks_ref[index, BLOCK:]
    normal, _ = group_norm(outputs_ref[...], pair.same)
    rate = sigmoid(offset[0:1] + upa_ref[...])
    values = values_ref[...]
    mixed = values + (first_ref[...].astype(F32) - values) * sigmoid(offset[1:2] + upv_ref[...])
    new_keys = keys_ref[...] * (1.0 + (rate - 1.0) * scale[1:2])
    bonus = head_sum(rec_ref[...] * new_keys * reward, pair.same)
    branch = (normal * scale[2:3] + offset[2:3] + bonus * mixed) * gate_ref[...]
    branch_ref[...] = branch.astype(BF)


def backward_local_kernel(
    heads, slope_ref, outputs_ref, read_ref, blocks_ref, rec_ref, keys_ref, values_ref, upa_ref, upv_ref, first_ref,
    gate_ref, scale_ref, offset_ref, reward_ref,
    local_ref, steps_ref, slope_out_ref, gate_out_ref, rec_out_ref, keys_out_ref, values_out_ref, sums_ref,
):
    pair = Pairing(heads, 3)
    same = pair.same
    count = rec_ref.shape[0] // BLOCK
    scale, offset, reward = scale_ref[...], offset_ref[...], reward_ref[...]
    normal, inverse = group_norm(outputs_ref[...], same)
    rate = sigmoid(offset[0:1] + upa_ref[...])
    values = values_ref[...]
    mixed = values + (first_ref[...].astype(F32) - values) * sigmoid(offset[1:2] + upv_ref[...])
    new_keys = keys_ref[...] * (1.0 + (rate - 1.0) * scale[1:2])
    rec = rec_ref[...]
    bonus = head_sum(rec * new_keys * reward, same)
    slope = slope_ref[...]
    gate_out_ref[...] = (slope * (normal * scale[2:3] + offset[2:3] + bonus * mixed)).astype(BF)
    inner = slope * gate_ref[...]
    d_bonus = head_sum(inner * mixed, same)
    rec_out_ref[...] = d_bonus * new_keys * reward
    keys_out_ref[...] = d_bonus * rec * reward
    values_out_ref[...] = inner * bonus
    d_normal = inner * scale[2:3]
    mean_a = head_sum(d_normal, same) * (1.0 / HEAD_SIZE)
    mean_b = head_sum(d_normal * normal, same) * (1.0 / HEAD_SIZE)
    slope_out_ref[...] = inverse * (d_normal - mean_a - normal * mean_b)
    sums_ref[0:1] = jnp.sum(inner * normal, axis=0, keepdims=True)
    sums_ref[1:2] = jnp.sum(inner, axis=0, keepdims=True)
    sums_ref[2:3] = jnp.sum(d_bonus * rec * new_keys, axis=0, keepdims=True)
    sums_ref[3:8] = jnp.zeros((5, slope.shape[1]), F32)
    total = None
    for index in range(count - 1, -1, -1):
        span = slice(index * BLOCK, (index + 1) * BLOCK)
        step = pair.tn(slope_out_ref[span], read_ref[span])
        steps_ref[index] = step
        total = step if total is None else pair.nt(total, pair.spread(blocks_ref[index, :BLOCK])) + step
    local_ref[...] = total


def backward_state_kernel(
    heads, moves_ref, locals_ref, flags_ref, states_ref, blocks_ref, steps_ref, inv_ref, wide_ref, fixed_ref, prb_ref, prk_ref,
    pak_ref, slope_ref, rec_extra_ref, keys_extra_ref, values_extra_ref, rec_ref, keys_ref, values_ref, upw_ref, upa_ref, upv_ref,
    first_ref, scale_ref, offset_ref, forget_ref,
    d_state_ref, d_rec_ref, d_keys_ref, d_values_ref, d_upw_ref, d_upa_ref, d_upv_ref, d_first_ref, sums_ref,
):
    pair = Pairing(heads, 3)
    same = pair.same
    width = heads * HEAD_SIZE
    rows, cols = side_iotas(width)
    strict, upto = rows > cols, rows >= cols
    count = rec_ref.shape[0] // BLOCK
    scale, offset, forget = scale_ref[...], offset_ref[...], forget_ref[...]
    outgoing = jnp.zeros((HEAD_SIZE, width), F32)
    for index in range(locals_ref.shape[0] - 1, -1, -1):
        moved = pair.nt(outgoing, pair.spread(moves_ref[index])) + locals_ref[index]
        outgoing = jnp.where(flags_ref[index : index + 1] > 0.0, moved, outgoing)
    row_ids = lax.broadcasted_iota(jnp.int32, (BLOCK, 2 * BLOCK), 0)
    col_ids = lax.broadcasted_iota(jnp.int32, (BLOCK, 2 * BLOCK), 1)
    later = ((col_ids < BLOCK) & (col_ids >= row_ids)) | (col_ids - BLOCK > row_ids)
    later = later.astype(BF)
    sums = [jnp.zeros((1, width), F32) for _ in range(5)]
    for index in range(count - 1, -1, -1):
        span = slice(index * BLOCK, (index + 1) * BLOCK)
        keys, values = keys_ref[span], values_ref[span]
        first = first_ref[span].astype(F32)
        sig_w, log_decay, rate, sig_v, mixed, inverse, unit, grown = prepared(
            keys, values, upw_ref[span], upa_ref[span], upv_ref[span],
            first, scale, offset, forget, same,
        )
        e_total, e_before, e_back, e_tail, e_last = decays(log_decay)
        beta, new_keys = unit * rate, keys * grown
        grown_r, grown_a = rec_ref[span] * e_total, -unit * e_before
        shrunk_b, shrunk_k = beta * e_back, new_keys * e_back
        tail_b, tail_k = beta * e_tail, new_keys * e_tail
        state, slope = states_ref[index], slope_ref[span]
        state_spread, outgoing_spread = pair.spread(state), pair.spread(outgoing)
        carried = pair.nt(wide_ref[span], state_spread) + fixed_ref[span]
        tails = pair.nt(jnp.concatenate([tail_b, tail_k], axis=0), outgoing_spread)
        d_carried = pair.tn(prb_ref[span], slope) + tails[:BLOCK]
        d_right = pair.tn(inv_ref[span], d_carried)
        slopes = jnp.concatenate([d_right, slope], axis=0)
        d_mixed = tails[BLOCK:] + values_extra_ref[span] + pair.tn(
            jnp.concatenate([pak_ref[span], prk_ref[span]], axis=0), slopes
        )
        d_grown = pair.nn(slopes, state_spread)
        on_c = pair.nt(slopes, pair.spread(carried))
        on_v = pair.nt(slopes, pair.spread(mixed))
        d_b = jnp.concatenate([jnp.where(strict, on_c[:BLOCK], 0.0), jnp.where(upto, on_c[BLOCK:], 0.0)], axis=0)
        d_k = jnp.concatenate([jnp.where(strict, on_v[:BLOCK], 0.0), jnp.where(upto, on_v[BLOCK:], 0.0)], axis=0)
        d_grown = d_grown + pair.nn(d_b, pair.spread(shrunk_b)) + pair.nn(d_k, pair.spread(shrunk_k))
        both = jnp.concatenate([grown_a, grown_r], axis=0)
        d_shrunk_b, d_shrunk_k = pair.tn(d_b, both), pair.tn(d_k, both)
        d_tails = pair.nn(jnp.concatenate([carried, mixed], axis=0), outgoing_spread)
        d_tail_b, d_tail_k = d_tails[:BLOCK], d_tails[BLOCK:]
        d_last = jnp.sum(state * outgoing, axis=0, keepdims=True) * e_last + jnp.sum(
            d_tail_b * tail_b + d_tail_k * tail_k, axis=0, keepdims=True
        )
        d_grown_a, d_grown_r = d_grown[:BLOCK], d_grown[BLOCK:]
        d_total = (
            d_grown_r * grown_r - d_shrunk_b * shrunk_b - d_shrunk_k * shrunk_k
            - d_tail_b * tail_b - d_tail_k * tail_k
        )
        d_log = exact_left(later, jnp.concatenate([d_total, d_grown_a * grown_a], axis=0)) + d_last
        d_rec_ref[span] = (d_grown_r * e_total + rec_extra_ref[span]).astype(BF)
        d_alpha = d_grown_a * e_before
        d_beta = d_shrunk_b * e_back + d_tail_b * e_tail
        d_new = d_shrunk_k * e_back + d_tail_k * e_tail + keys_extra_ref[span]
        d_unit = d_beta * rate - d_alpha
        d_rate = d_beta * unit + d_new * keys * scale[1:2]
        d_scaled = inverse * (d_unit - unit * head_sum(d_unit * unit, same))
        d_keys_ref[span] = (d_new * grown + d_scaled * scale[0:1]).astype(BF)
        d_upw = d_log * log_decay * (1.0 - sig_w)
        d_upa = d_rate * rate * (1.0 - rate)
        d_upv = d_mixed * (first - values) * sig_v * (1.0 - sig_v)
        d_upw_ref[span] = d_upw.astype(BF)
        d_upa_ref[span] = d_upa.astype(BF)
        d_upv_ref[span] = d_upv.astype(BF)
        d_values_ref[span] = (d_mixed * (1.0 - sig_v)).astype(BF)
        d_first_ref[span] = d_mixed * sig_v
        terms = (d_scaled * keys, d_new * keys * (rate - 1.0), d_upa, d_upv, d_upw)
        sums = [total + jnp.sum(term, axis=0, keepdims=True) for total, term in zip(sums, terms)]
        outgoing = pair.nt(outgoing, pair.spread(blocks_ref[index, :BLOCK])) + steps_ref[index]
    d_state_ref[...] = outgoing
    for index in range(5):
        sums_ref[index : index + 1] = sums[index]
    sums_ref[5:8] = jnp.zeros((3, width), F32)


def local_call(body, heads, results, operands):
    return pl.pallas_call(
        functools.partial(body, heads),
        out_shape=tuple(jax.ShapeDtypeStruct(shape, dtype) for shape, dtype in results),
        in_specs=[pl.BlockSpec(memory_space=pltpu.VMEM)] * len(operands),
        out_specs=tuple(pl.BlockSpec(memory_space=pltpu.VMEM) for _ in results),
        compiler_params=pltpu.CompilerParams(vmem_limit_bytes=48 * 1024 * 1024),
    )(*operands)


TILE = 256


def store_split(refs, span, value):
    high = value.astype(BF)
    refs[0][span] = high
    if len(refs) > 1:
        refs[1][span] = (value - high.astype(F32)).astype(BF)


def over_tiles(rows, body, start=None):
    tile = min(TILE, rows)
    carry = jnp.zeros((1, 1), F32) if start is None else start
    step = lambda index, total: body(pl.ds(pl.multiple_of(index * tile, tile), tile), index * tile, total)
    return lax.fori_loop(0, rows // tile, step, carry, unroll=math.gcd(2, rows // tile))


def tile_dot(left, span, right, kind):
    total = dot_kind(left[0][span], right[0][...], kind)
    if len(left) > 1:
        total = total + dot_kind(left[0][span], right[1][...], kind)
        total = total + dot_kind(left[1][span], right[0][...], kind)
    return total


def total_of(value):
    return jnp.sum(jnp.sum(value, axis=0, keepdims=True), axis=1, keepdims=True)


def diagonal(shape, first_row):
    rows = lax.broadcasted_iota(jnp.int32, shape, 0) + first_row
    return rows == lax.broadcasted_iota(jnp.int32, shape, 1)


def expansion(shift):
    value = COEFF_A + COEFF_B * shift + COEFF_C * shift * shift
    return value, COEFF_B + 2.0 * COEFF_C * shift


def newton_square_kernel(
    coarse, active_ref, x_ref, out_ref, x_high, x_low, d_high, d_low, b_high, b_low, rest_ref
):
    rows = out_ref.shape[0]
    parts, halves, half_rows, width = x_ref.shape

    def advance(step, norm, fine):
        now = step % 2
        xs, fresh_xs = [(x_high.at[index], x_low.at[index]) for index in (now, 1 - now)]
        ds, bs = (d_high, d_low), (b_high, b_low)
        if not fine:
            xs, ds, bs = xs[:1], ds[:1], bs[:1]
        shift = norm * (1.0 / rows)
        value, slope = expansion(shift)

        def gram(span, first, total):
            product = tile_dot(xs, span, xs, "nt")
            rest = jnp.where(diagonal(product.shape, first), product - shift, product)
            rest_ref[span] = rest
            store_split(ds, span, rest)
            return total

        def terms(span, first, total):
            store_split(bs, span, slope * rest_ref[span] + COEFF_C * tile_dot(ds, span, ds, "nn"))
            return total

        def update(span, first, total):
            fresh = value * out_ref[span] + tile_dot(bs, span, xs, "nn")
            out_ref[span] = fresh
            store_split(fresh_xs, span, fresh)
            return total + total_of(jnp.square(fresh))

        over_tiles(rows, gram)
        over_tiles(rows, terms)
        return over_tiles(rows, update)

    def iterate():
        def begin(span, first, total):
            for half in range(halves):
                for part in range(parts):
                    tile = x_ref[part, half, span]
                    place = pl.ds(
                        pl.multiple_of(half * half_rows + first, min(TILE, half_rows)), tile.shape[0]
                    )
                    out_ref[place, part * width : (part + 1) * width] = tile
                    total = total + total_of(jnp.square(tile))
            return total

        norm = over_tiles(half_rows, begin)
        scale = 1.0 / (jnp.sqrt(norm) + 1e-07)

        def normalise(span, first, total):
            fresh = out_ref[span] * scale
            out_ref[span] = fresh
            store_split((x_high.at[0], x_low.at[0]), span, fresh)
            return total

        over_tiles(rows, normalise)
        norm = norm * scale * scale
        norm = lax.fori_loop(0, coarse, lambda step, norm: advance(step, norm, False), norm)
        lax.fori_loop(coarse, NS_STEPS, lambda step, norm: advance(step, norm, True), norm)

    pl.when(active_ref[0] > 0)(iterate)


def newton_wide_kernel(
    coarse, active_ref, gram_ref, key_ref, value_ref, out_ref,
    x_high, d_high, d_low, b_high, b_low, r_high, r_low, a_ref, terms_ref, square_ref,
):
    rows = key_ref.shape[0]

    def trace_of(tile, first):
        return total_of(jnp.where(diagonal(tile.shape, first), tile, 0.0))

    def without(tile, first, shift):
        return jnp.where(diagonal(tile.shape, first), tile - shift, tile)

    def advance(step, trace, fine, last=False):
        now = step % 2
        xs, fresh_xs = (x_high.at[now],), (x_high.at[1 - now],)
        ds, bs, rs = (d_high, d_low), (b_high, b_low), (r_high, r_low)
        if not fine:
            ds, bs, rs = ds[:1], bs[:1], rs[:1]
        shift = trace * (1.0 / rows)
        value, slope = expansion(shift)

        def terms(span, first, total):
            fresh = slope * without(a_ref[span], first, shift)
            fresh = fresh + COEFF_C * tile_dot(ds, span, ds, "nn")
            terms_ref[span] = fresh
            store_split(bs, span, fresh)
            return total

        def update(span, first, total):
            fresh = value * out_ref[span] + tile_dot(bs[:1], span, xs, "nn")
            out_ref[span] = fresh
            if not last:
                store_split(fresh_xs, span, fresh)
            return total

        def square(span, first, total):
            fresh = 2.0 * value * terms_ref[span] + tile_dot(bs, span, bs, "nn")
            square_ref[span] = fresh
            store_split(rs, span, fresh)
            return total + total_of(fresh * a_ref[span])

        over_tiles(rows, terms)
        over_tiles(rows, update)
        if last:
            return trace
        fresh_trace = value * value * trace + over_tiles(rows, square)
        fresh_shift = fresh_trace * (1.0 / rows)

        def move(span, first, total):
            fresh = value * value * a_ref[span] + shift * square_ref[span]
            fresh = fresh + tile_dot(ds, span, rs, "nn")
            a_ref[span] = fresh
            store_split((d_high, d_low), span, without(fresh, first, fresh_shift))
            return total

        over_tiles(rows, move)
        return fresh_trace

    def iterate():
        trace = over_tiles(rows, lambda span, first, total: total + trace_of(gram_ref[span], first))
        scale = 1.0 / (jnp.sqrt(trace) + 1e-07)
        trace = trace * scale * scale
        first_shift = trace * (1.0 / rows)

        def begin(span, first, total):
            @pl.when(active_ref[0] == 1)
            def _():
                out_ref[span] = key_ref[span]

            @pl.when(active_ref[0] == 2)
            def _():
                out_ref[span] = value_ref[:, span].T

            fresh = out_ref[span] * scale
            out_ref[span] = fresh
            store_split((x_high.at[0],), span, fresh)
            tile = gram_ref[span] * (scale * scale)
            a_ref[span] = tile
            store_split((d_high, d_low), span, without(tile, first, first_shift))
            return total

        over_tiles(rows, begin)
        trace = lax.fori_loop(0, coarse, lambda step, trace: advance(step, trace, False), trace)
        trace = lax.fori_loop(
            coarse, NS_STEPS - 1, lambda step, trace: advance(step, trace, True), trace
        )
        advance(NS_STEPS - 1, trace, False, True)

    pl.when(active_ref[0] > 0)(iterate)


def newton_call(body, active, operands, result_shape, scratch):
    return pl.pallas_call(
        body,
        out_shape=jax.ShapeDtypeStruct(result_shape, F32),
        in_specs=[pl.BlockSpec(memory_space=pltpu.SMEM)]
        + [pl.BlockSpec(memory_space=pltpu.VMEM)] * len(operands),
        out_specs=pl.BlockSpec(memory_space=pltpu.VMEM),
        scratch_shapes=[pltpu.VMEM(shape, dtype) for shape, dtype in scratch],
        cost_estimate=pl.CostEstimate(
            flops=2 * 30 * result_shape[0] ** 2 * result_shape[1],
            bytes_accessed=8 * result_shape[0] * result_shape[1],
            transcendentals=0,
        ),
        compiler_params=pltpu.CompilerParams(vmem_limit_bytes=58 * 1024 * 1024),
    )(active.astype(jnp.int32).reshape(1), *operands)


def newton_square(active, whole):
    shape = (whole.shape[1] * whole.shape[2], whole.shape[0] * whole.shape[3])
    scratch = [((2, *shape), BF)] * 2 + [(shape, BF)] * 4 + [(shape, F32)]
    return newton_call(
        functools.partial(newton_square_kernel, 3), active, (whole,), shape, scratch
    )


def newton_wide(active, gram, key, value):
    part = key
    scratch = [((2, *part.shape), BF)] + [(gram.shape, BF)] * 6 + [(gram.shape, F32)] * 3
    return newton_call(
        functools.partial(newton_wide_kernel, 2), active, (gram, key, value), part.shape, scratch
    )


LOWRANK_PASSES = (1, 3, 3, 3, 3)


def newton_small_kernel(active_ref, gram_ref, member_ref, out_ref):
    def iterate():
        member = member_ref[...]
        rows = lax.broadcasted_iota(jnp.int32, member.shape, 0)
        eye = (rows == lax.broadcasted_iota(jnp.int32, member.shape, 1)).astype(F32)
        sizes = jnp.maximum(jnp.sum(member, axis=1, keepdims=True), 1.0)

        def block_total(gram):
            return jnp.sum(jnp.sum(gram * eye, axis=0, keepdims=True) * member, axis=1, keepdims=True)

        def dot(a, b, fine):
            a_high, a_low = split(a)
            b_high, b_low = split(b)
            total = dot_kind(a_high, b_high, "nn")
            if fine:
                total = total + (dot_kind(a_high, b_low, "nn") + dot_kind(a_low, b_high, "nn"))
            return total

        grams, currents = [], []
        for index in range(gram_ref.shape[0]):
            gram = gram_ref[index] * member
            scale = 1.0 / (jnp.sqrt(block_total(gram)) + 1e-07)
            grams.append(gram * (scale * scale))
            currents.append(eye * scale)
        for step in range(NS_STEPS):
            fine = LOWRANK_PASSES[step] > 1
            for index, gram in enumerate(grams):
                shift = block_total(gram) / sizes
                value, slope = expansion(shift)
                rest = gram - shift * eye
                terms = slope * rest + COEFF_C * dot(rest, rest, fine)
                currents[index] = value * currents[index] + dot(terms, currents[index], fine)
                if step < NS_STEPS - 1:
                    square = 2.0 * value * terms + dot(terms, terms, fine)
                    grams[index] = value * value * gram + shift * square + dot(rest, square, fine)
        for index, current in enumerate(currents):
            out_ref[index] = current

    pl.when(active_ref[0] > 0)(iterate)


def newton_small(active, gram, member):
    return pl.pallas_call(
        newton_small_kernel,
        out_shape=jax.ShapeDtypeStruct(gram.shape, F32),
        in_specs=[pl.BlockSpec(memory_space=pltpu.SMEM)]
        + [pl.BlockSpec(memory_space=pltpu.VMEM)] * 2,
        out_specs=pl.BlockSpec(memory_space=pltpu.VMEM),
        cost_estimate=pl.CostEstimate(
            flops=2 * 100 * gram.shape[1] ** 3, bytes_accessed=0, transcendentals=0
        ),
        compiler_params=pltpu.CompilerParams(vmem_limit_bytes=48 * 1024 * 1024),
    )(active.astype(jnp.int32).reshape(1), gram, member)


MESH = pl.DeviceIdType.MESH


def greet(neighbours):
    barrier = pltpu.get_barrier_semaphore()
    for there, device in neighbours:
        @pl.when(there)
        def _():
            pl.semaphore_signal(barrier, inc=1, device_id=device, device_id_type=MESH)

    pl.semaphore_wait(barrier, sum(jnp.where(there, 1, 0) for there, _ in neighbours))


def line_sum_kernel(count, pieces, *refs):
    me = lax.axis_index("head")
    greet([(me > 0, {"head": me - 1}), (me < count - 1, {"head": me + 1})])
    line_sum_body(count, pieces, *refs)


def line_sum_body(
    count, pieces, x_ref, out_ref, right_in, left_in, right_out, left_out,
    right_send, right_recv, left_send, left_recv, on_send, on_recv, back_send, back_recv,
):
    me = lax.axis_index("head")
    rows = x_ref.shape[0] // (count * pieces)
    right, left = {"head": me + 1}, {"head": me - 1}

    def span(slot):
        return pl.ds(pl.multiple_of(slot * rows, rows), rows)

    def reduce_copy(slot, to_right, source):
        arrive, send, recv, device = (
            (right_in, right_send, right_recv, right)
            if to_right
            else (left_in, left_send, left_recv, left)
        )
        return pltpu.make_async_remote_copy(
            src_ref=source, dst_ref=arrive.at[slot], send_sem=send.at[slot],
            recv_sem=recv.at[slot], device_id=device, device_id_type=MESH,
        )

    def share_copy(slot, to_right):
        send, recv, device = (on_send, on_recv, right) if to_right else (back_send, back_recv, left)
        return pltpu.make_async_remote_copy(
            src_ref=out_ref.at[span(slot)], dst_ref=out_ref.at[span(slot)], send_sem=send.at[slot],
            recv_sem=recv.at[slot], device_id=device, device_id_type=MESH,
        )

    def pass_on(slot, to_right, first):
        arrive, leave = (right_in, right_out) if to_right else (left_in, left_out)

        @pl.when(first)
        def _():
            reduce_copy(slot, to_right, x_ref.at[span(slot)]).start()

        @pl.when(jnp.logical_not(first))
        def _():
            reduce_copy(slot, to_right, x_ref.at[span(slot)]).wait_recv()
            leave[slot] = x_ref[span(slot)] + arrive[slot]
            reduce_copy(slot, to_right, leave.at[slot]).start()

    for far in range(count - 1):
        for piece in range(pieces):
            owner = count - 1 - far

            @pl.when(me < owner)
            def _():
                pass_on(owner * pieces + piece, True, me == 0)

            @pl.when(me > far)
            def _():
                pass_on(far * pieces + piece, False, me == count - 1)

    for piece in range(pieces):
        slot = me * pieces + piece
        out_ref[span(slot)] = x_ref[span(slot)]

        @pl.when(me > 0)
        def _():
            reduce_copy(slot, True, x_ref.at[span(slot)]).wait_recv()
            out_ref[span(slot)] += right_in[slot]

        @pl.when(me < count - 1)
        def _():
            reduce_copy(slot, False, x_ref.at[span(slot)]).wait_recv()
            out_ref[span(slot)] += left_in[slot]
            share_copy(slot, True).start()

        @pl.when(me > 0)
        def _():
            share_copy(slot, False).start()

    for far in range(1, count):
        for piece in range(pieces):
            @pl.when(me >= far)
            def _():
                copy = share_copy((me - far) * pieces + piece, True)
                copy.wait_recv()
                pl.when(me < count - 1)(copy.start)

            @pl.when(me + far < count)
            def _():
                copy = share_copy((me + far) * pieces + piece, False)
                copy.wait_recv()
                pl.when(me > 0)(copy.start)

    for slot in range(count * pieces):
        owner = slot // pieces
        pl.when(me < owner)(lambda: reduce_copy(slot, True, x_ref.at[span(slot)]).wait_send())
        pl.when(me > owner)(lambda: reduce_copy(slot, False, x_ref.at[span(slot)]).wait_send())
        pl.when((owner <= me) & (me < count - 1))(lambda: share_copy(slot, True).wait_send())
        pl.when((owner >= me) & (me > 0))(lambda: share_copy(slot, False).wait_send())


def line_sum(value, collective_id, pieces=2):
    count = lax.axis_size("head")
    slots = count * pieces
    buffer = pltpu.VMEM((slots, value.shape[0] // slots, value.shape[1]), F32)
    return pl.pallas_call(
        functools.partial(line_sum_kernel, count, pieces),
        out_shape=jax.ShapeDtypeStruct(value.shape, F32),
        in_specs=[pl.BlockSpec(memory_space=pltpu.VMEM)],
        out_specs=pl.BlockSpec(memory_space=pltpu.VMEM),
        scratch_shapes=[buffer] * 4 + [pltpu.SemaphoreType.DMA((slots,))] * 8,
        compiler_params=pltpu.CompilerParams(collective_id=collective_id, has_side_effects=True),
    )(value)


def plane_places():
    me = lax.axis_index("seq")
    core = me % 2
    return me // 2, core, {"seq": me + 1 - 2 * core}, lambda pair: {"seq": 2 * pair + core}


def plane_reduce_steps(pairs, x_ref, out_ref, near_in, total_ref, far_in, near_send, near_recv, far_send, far_recv):
    pair, core, partner, like = plane_places()
    order = [(pair + step) % pairs for step in range(1, pairs)]

    def near(part):
        return pltpu.make_async_remote_copy(
            src_ref=x_ref.at[part, 1 - core], dst_ref=near_in.at[part], send_sem=near_send.at[part],
            recv_sem=near_recv.at[part], device_id=partner, device_id_type=MESH,
        )

    def far(part, source):
        return pltpu.make_async_remote_copy(
            src_ref=total_ref.at[part], dst_ref=far_in.at[source], send_sem=far_send.at[part],
            recv_sem=far_recv.at[source], device_id=like(part), device_id_type=MESH,
        )

    def begin():
        for part in order + [pair]:
            near(part).start()
        for part in order:
            near(part).wait_recv()
            total_ref[part] = x_ref[part, core] + near_in[part]
            far(part, pair).start()
        near(pair).wait_recv()
        out_ref[...] = x_ref[pair, core] + near_in[pair]

    def finish():
        for source in order:
            far(source, source).wait_recv()
            out_ref[...] += far_in[source]
        for part in order + [pair]:
            near(part).wait_send()
        for part in order:
            far(part, pair).wait_send()

    return begin, finish


def greet_all(pairs, neighbours):
    pair, core, partner, like = plane_places()
    always = pair >= 0
    plane = [(always, partner)]
    plane += [(always, like((pair + far) % pairs)) for far in range(1, pairs)]
    greet(plane + neighbours)


def reduce_and_sum_kernel(pairs, count, pieces, parts_ref, line_ref, own_ref, sum_ref, *scratch):
    line = lax.axis_index("head")
    greet_all(
        pairs, [(line > 0, {"head": line - 1}), (line < count - 1, {"head": line + 1})]
    )
    begin, finish = plane_reduce_steps(pairs, parts_ref, own_ref, *scratch[:7])
    begin()
    line_sum_body(count, pieces, line_ref, sum_ref, *scratch[7:])
    finish()


def reduce_and_sum(parts, line_value, collective_id, pieces=2):
    pairs, shape = parts.shape[0], parts.shape[2:]
    count = lax.axis_size("head")
    slots = count * pieces
    rows, columns = line_value.shape
    return pl.pallas_call(
        functools.partial(reduce_and_sum_kernel, pairs, count, pieces),
        out_shape=(
            jax.ShapeDtypeStruct(shape, F32),
            jax.ShapeDtypeStruct(line_value.shape, F32),
        ),
        in_specs=[pl.BlockSpec(memory_space=pltpu.VMEM)] * 2,
        out_specs=(pl.BlockSpec(memory_space=pltpu.VMEM), pl.BlockSpec(memory_space=pltpu.VMEM)),
        scratch_shapes=[pltpu.VMEM((pairs, *shape), F32)] * 3
        + [pltpu.SemaphoreType.DMA((pairs,))] * 4
        + [pltpu.VMEM((slots, rows // slots, columns), F32)] * 4
        + [pltpu.SemaphoreType.DMA((slots,))] * 8,
        compiler_params=pltpu.CompilerParams(
            collective_id=collective_id, has_side_effects=True, vmem_limit_bytes=48 * 1024 * 1024
        ),
    )(parts, line_value)


def share_gather_kernel(
    pairs, count, pieces, square_ref, small_ref, gram_ref, shared_ref, whole_ref, full_ref,
    out_send, in_recv, back_send, back_recv, half_send, half_recv, gram_send, gram_recv,
    right_send, right_recv, left_send, left_recv, local_sem,
):
    pair, core, partner, like = plane_places()
    line = lax.axis_index("head")
    right, left = {"head": line + 1}, {"head": line - 1}
    half_rows = square_ref.shape[0]
    rows = half_rows // pieces
    gathers = core == 0
    owners = min(pairs, 4)
    kind = pair % 2
    slot = (pair // 2) * 2 + core
    takes = (core == 1) & (pair < owners)

    def odd(other):
        return {"seq": 2 * other + 1}

    def even(other):
        return {"seq": 2 * other}

    neighbours = [(gathers & (line > 0), left), (gathers & (line < count - 1), right)]
    for step in range(owners // 2):
        target = kind + 2 * step
        neighbours.append(((core == 0) & (target != pair), odd(target)))
    for step in range(pairs // 2):
        source = kind + 2 * step
        neighbours.append((takes & (source != pair), even(source)))
    greet_all(pairs, neighbours)

    def gram_copy(source_slot, target):
        return pltpu.make_async_remote_copy(
            src_ref=gram_ref, dst_ref=full_ref.at[source_slot], send_sem=gram_send.at[target // 2],
            recv_sem=gram_recv.at[source_slot], device_id=odd(target), device_id_type=MESH,
        )

    def half_copy():
        return pltpu.make_async_remote_copy(
            src_ref=square_ref, dst_ref=whole_ref.at[line, 1], send_sem=half_send.at[0],
            recv_sem=half_recv.at[0], device_id=partner, device_id_type=MESH,
        )

    def out_copy(part):
        return pltpu.make_async_remote_copy(
            src_ref=small_ref, dst_ref=shared_ref.at[pair, core], send_sem=out_send.at[part],
            recv_sem=in_recv.at[pair], device_id=like(part), device_id_type=MESH,
        )

    def in_copy(source):
        return pltpu.make_async_remote_copy(
            src_ref=small_ref, dst_ref=shared_ref.at[source, core], send_sem=out_send.at[source],
            recv_sem=in_recv.at[source], device_id=like(source), device_id_type=MESH,
        )

    def partner_copy(source, side, source_ref):
        return pltpu.make_async_remote_copy(
            src_ref=source_ref, dst_ref=shared_ref.at[source, side], send_sem=back_send.at[source],
            recv_sem=back_recv.at[source], device_id=partner, device_id_type=MESH,
        )

    def span(piece):
        return pl.ds(piece * rows, rows)

    def line_copy(owner, half, piece, to_right, source):
        send, recv, device = (
            (right_send, right_recv, right) if to_right else (left_send, left_recv, left)
        )
        return pltpu.make_async_remote_copy(
            src_ref=source, dst_ref=whole_ref.at[owner, half, span(piece)],
            send_sem=send.at[owner, half, piece], recv_sem=recv.at[owner, half, piece],
            device_id=device, device_id_type=MESH,
        )

    order = [(pair + step) % pairs for step in range(1, pairs)]
    pl.when(core == 1)(lambda: half_copy().start())
    for step in range(owners // 2):
        target = kind + 2 * step
        pl.when((core == 0) | (target != pair))(lambda: gram_copy(slot, target).start())
    for part in order:
        out_copy(part).start()
    partner_copy(pair, core, small_ref).start()
    shared_ref[pair, core] = small_ref[...]
    own_gram = pltpu.make_async_copy(gram_ref, full_ref.at[slot], local_sem)
    pl.when(takes)(own_gram.start)

    def gather():
        whole_ref[line, 0] = square_ref[...]
        half_copy().wait_recv()
        for half in range(2):
            for piece in range(pieces):
                own = whole_ref.at[line, half, span(piece)]
                pl.when(line < count - 1)(lambda: line_copy(line, half, piece, True, own).start())
                pl.when(line > 0)(lambda: line_copy(line, half, piece, False, own).start())
        for far in range(1, count):
            for half in range(2):
                for piece in range(pieces):
                    for there, end, owner, to_right in (
                        (line >= far, line == count - 1, line - far, True),
                        (line + far < count, line == 0, line + far, False),
                    ):
                        @pl.when(there)
                        def _():
                            copy = line_copy(
                                owner, half, piece, to_right, whole_ref.at[owner, half, span(piece)]
                            )
                            copy.wait_recv()
                            pl.when(jnp.logical_not(end))(copy.start)

        for owner in range(count):
            for half in range(2):
                for piece in range(pieces):
                    sent = whole_ref.at[owner, half, span(piece)]
                    pl.when((owner <= line) & (line < count - 1))(
                        lambda: line_copy(owner, half, piece, True, sent).wait_send()
                    )
                    pl.when((owner >= line) & (line > 0))(
                        lambda: line_copy(owner, half, piece, False, sent).wait_send()
                    )

    pl.when(gathers)(gather)
    for source in order:
        in_copy(source).wait_recv()
        partner_copy(source, core, shared_ref.at[source, core]).start()

    def take():
        own_gram.wait()
        for step in range(pairs // 2):
            for side in range(2):
                source = kind + 2 * step
                pl.when((side == 0) | (source != pair))(
                    lambda: gram_copy(2 * step + side, pair).wait_recv()
                )

    pl.when(takes)(take)
    for source in order + [pair]:
        partner_copy(source, 1 - core, small_ref).wait_recv()
    for source in order + [pair]:
        partner_copy(source, core, small_ref).wait_send()
    for part in order:
        out_copy(part).wait_send()
    pl.when(core == 1)(lambda: half_copy().wait_send())
    for step in range(owners // 2):
        target = kind + 2 * step
        pl.when((core == 0) | (target != pair))(lambda: gram_copy(slot, target).wait_send())


def share_gather(square, small, gram, collective_id, pieces=2):
    pairs, count = lax.axis_size("seq") // 2, lax.axis_size("head")
    slots = (count, 2, pieces)
    results = ((pairs, 2, *small.shape), (count, 2, *square.shape), (pairs, *gram.shape))
    dma = pltpu.SemaphoreType.DMA
    return pl.pallas_call(
        functools.partial(share_gather_kernel, pairs, count, pieces),
        out_shape=tuple(jax.ShapeDtypeStruct(shape, F32) for shape in results),
        in_specs=[pl.BlockSpec(memory_space=pltpu.VMEM)] * 3,
        out_specs=tuple(pl.BlockSpec(memory_space=pltpu.VMEM) for _ in results),
        scratch_shapes=[dma((pairs,))] * 4 + [dma((1,))] * 2 + [dma((2,)), dma((pairs,))]
        + [dma(slots)] * 4 + [dma],
        compiler_params=pltpu.CompilerParams(
            collective_id=collective_id, has_side_effects=True, vmem_limit_bytes=48 * 1024 * 1024
        ),
    )(square, small, gram)


def gram_part_kernel(which_ref, key_ref, value_ref, out_ref):
    rows = out_ref.shape[0]
    start = pl.multiple_of(which_ref[1] * rows, rows)

    def three(left, right, kind):
        left, right = split(left), split(right)
        total = dot_kind(left[0], right[0], kind)
        return total + (dot_kind(left[0], right[1], kind) + dot_kind(left[1], right[0], kind))

    @pl.when(which_ref[0] == 0)
    def _():
        out_ref[...] = three(key_ref[pl.ds(start, rows)], key_ref[...], "nt")

    @pl.when(which_ref[0] == 1)
    def _():
        out_ref[...] = three(value_ref[:, pl.ds(start, rows)], value_ref[...], "tn")


def gram_rows(kind, part, parts, key, value):
    return pl.pallas_call(
        gram_part_kernel,
        out_shape=jax.ShapeDtypeStruct((key.shape[0] // parts, key.shape[0]), F32),
        in_specs=[pl.BlockSpec(memory_space=pltpu.SMEM)]
        + [pl.BlockSpec(memory_space=pltpu.VMEM)] * 2,
        out_specs=pl.BlockSpec(memory_space=pltpu.VMEM),
        compiler_params=pltpu.CompilerParams(vmem_limit_bytes=48 * 1024 * 1024),
    )(jnp.stack([kind, part]).astype(jnp.int32), key, value)


def exact(left, right):
    return jnp.matmul(left, right, precision=HIGHEST, preferred_element_type=F32)


def close(left, right):
    return jnp.dot(left, right, precision=lax.Precision.HIGH, preferred_element_type=F32)


def after(value, *others):
    return lax.optimization_barrier((value, *others))[0]


def pair_swap(value):
    count = lax.axis_size("seq")
    return lax.ppermute(value, "seq", [(index, index ^ 1) for index in range(count)])


def pair_halves(value, core):
    mine = lax.dynamic_index_in_dim(value, core, 0, keepdims=False)
    other = lax.dynamic_index_in_dim(value, 1 - core, 0, keepdims=False)
    return mine + pair_swap(other)


def pair_whole(mine, core):
    other = pair_swap(mine)
    first = core == 0
    return jnp.stack([jnp.where(first, mine, other), jnp.where(first, other, mine)])


def across_pairs(value):
    count = lax.axis_size("seq")
    groups = [list(range(core, count, 2)) for core in range(2)]
    return lax.all_to_all(value, "seq", 0, 0, tiled=True, axis_index_groups=groups)


def to_all_pairs(value, pairs):
    return across_pairs(jnp.broadcast_to(value[None], (pairs, *value.shape)))


def on_device(
    input_embeddings,
    loss_adjoint,
    earliest_tier_content,
    opening_memory,
    live_extents,
    lagged_blend_coeffs,
    standardize_scales,
    standardize_offsets,
    adapter_narrowing_coeffs,
    adapter_widening_coeffs,
    attention_scale_lines,
    attention_offset_lines,
    present_reward_array,
    forgetting_offset,
    readin_maps,
    emission_coeffs,
    feedforward_address_coeffs,
    feedforward_content_coeffs,
    lagged_blend_velocity,
    standardize_scale_velocity,
    standardize_offset_velocity,
    narrowing_velocity,
    widening_velocity,
    attention_scale_velocity,
    attention_offset_velocity,
    reward_velocity_array,
    forgetting_velocity,
    readin_velocity,
    emission_velocity,
    feedforward_address_velocity,
    feedforward_content_velocity,
):
    seq_count = lax.axis_size("seq")
    seq_index = lax.axis_index("seq")
    overall_tally = input_embeddings.shape[0]
    stride = live_extents.shape[0]
    per_sequence = seq_count // stride
    place = seq_index // stride
    sequence_id = seq_index % stride
    is_first = place == 0
    is_last = place == per_sequence - 1
    slot_ids = place * overall_tally + lax.iota(jnp.int32, overall_tally)
    live = (slot_ids < live_extents[sequence_id]).astype(jnp.float32)[:, None]
    sequence_edges = (
        0,
        LOWRANK_DECAY,
        LOWRANK_DECAY + LOWRANK_RATE,
        LOWRANK_DECAY + LOWRANK_RATE + LOWRANK_VALUE,
        LOWRANK_DECAY + LOWRANK_RATE + LOWRANK_VALUE + LOWRANK_GATE,
    )
    sequence_spans = list(zip(sequence_edges[:-1], sequence_edges[1:]))
    sources = (1, 4, 3, 5)
    inputs = input_embeddings.astype(jnp.float32)
    normed, first_pull = jax.vjp(layer_norm, inputs, standardize_scales[0], standardize_offsets[0])
    before = jnp.concatenate([from_before(normed[-1:], is_first, stride), normed[:-1]], axis=0)
    delta = before - normed
    mixes = [
        (normed + delta * lagged_blend_coeffs[index]).astype(jnp.bfloat16) for index in range(6)
    ]
    weights = readin_maps.astype(jnp.bfloat16)
    down_matrix = adapter_narrowing_coeffs.astype(jnp.bfloat16)
    up_matrix = adapter_widening_coeffs.astype(jnp.bfloat16)
    acceptance_lines = product(mixes[0], weights[0])
    address_lines = product(mixes[2], weights[1])
    content_lines = product(mixes[3], weights[2])
    hidden = [
        product(
            mixes[sources[index]],
            down_matrix[:, sequence_spans[index][0] : sequence_spans[index][1]],
        )
        for index in range(4)
    ]
    tanh_w = jnp.tanh(hidden[0])
    gate_sig = jax.nn.sigmoid(hidden[3])
    acts = [
        tanh_w.astype(jnp.bfloat16),
        hidden[1].astype(jnp.bfloat16),
        hidden[2].astype(jnp.bfloat16),
        gate_sig.astype(jnp.bfloat16),
    ]
    widened_lines = [
        product(acts[index], up_matrix[sequence_spans[index][0] : sequence_spans[index][1]])
        for index in range(4)
    ]
    width = acceptance_lines.shape[1]
    local_heads = width // HEAD_SIZE
    blocks_count = overall_tally // BLOCK
    lines = ((overall_tally, width), F32)
    low_lines = ((overall_tally, width), BF)
    tiny = ((8, width), F32)
    state_shape = ((HEAD_SIZE, width), F32)
    steps_shape = ((blocks_count, HEAD_SIZE, width), F32)
    pieces_shape = ((blocks_count, 2 * HEAD_SIZE, width), F32)
    reward_row = present_reward_array.reshape(1, width)
    forget_row = forgetting_offset.reshape(1, width)
    raw_lines = (address_lines, content_lines)
    summary, pieces, read, local, solved, wide, fixed, pair_rb, pair_rk, pair_ak = local_call(
        forward_local_kernel,
        local_heads,
        [((2 * HEAD_SIZE, width), F32), pieces_shape] + [lines] * 8,
        (acceptance_lines, *raw_lines, *widened_lines[:3], earliest_tier_content)
        + (attention_scale_lines, attention_offset_lines, forget_row),
    )
    distances = range(1, per_sequence)
    earlier = jnp.stack([passed_along(summary, "seq", far * stride) for far in distances][::-1])
    later_moves = jnp.stack(
        [passed_along(summary[:HEAD_SIZE], "seq", -far * stride) for far in distances]
    )
    earlier_flags = jnp.stack([(place >= far).astype(F32) for far in distances][::-1])
    later_flags = jnp.stack([(place + far < per_sequence).astype(F32) for far in distances])
    earlier_flags = jnp.broadcast_to(earlier_flags[:, None], (per_sequence - 1, width))
    later_flags = jnp.broadcast_to(later_flags[:, None], (per_sequence - 1, width))
    own_start = lax.dynamic_index_in_dim(opening_memory, sequence_id, 0, keepdims=False)
    own_start = jnp.swapaxes(own_start, 0, 1).reshape(HEAD_SIZE, width)
    adapter_result, states, outputs = local_call(
        forward_state_kernel,
        local_heads,
        [low_lines, steps_shape, lines],
        (own_start, earlier, earlier_flags, pieces, read, local, acceptance_lines, *raw_lines)
        + (widened_lines[1], widened_lines[2], earliest_tier_content, widened_lines[3])
        + (attention_scale_lines, attention_offset_lines, reward_row),
    )
    out_low = emission_coeffs.astype(jnp.bfloat16)
    attended = inputs + line_sum(product(adapter_result, out_low), 1)
    normed_two, second_pull = jax.vjp(
        layer_norm, attended, standardize_scales[1], standardize_offsets[1]
    )
    before_two = jnp.concatenate(
        [from_before(normed_two[-1:], is_first, stride), normed_two[:-1]], axis=0
    )
    delta_two = before_two - normed_two
    key_in = (normed_two + delta_two * lagged_blend_coeffs[6]).astype(jnp.bfloat16)
    keys_low = feedforward_address_coeffs.astype(jnp.bfloat16)
    values_low = feedforward_content_coeffs.astype(jnp.bfloat16)
    hidden_ffn = product(key_in, keys_low)
    activated = jnp.square(jax.nn.relu(hidden_ffn)).astype(jnp.bfloat16)
    grad_result = loss_adjoint.astype(jnp.float32) * live
    grad_low = grad_result.astype(jnp.bfloat16)
    grad_ffnvalue = inner_rows(activated, grad_low)
    grad_hidden = (outer_back(grad_low, values_low) * 2.0 * jax.nn.relu(hidden_ffn)).astype(
        jnp.bfloat16
    )
    grad_ffnkey = inner_rows(key_in, grad_hidden)
    pairs, core, pair = seq_count // 2, seq_index % 2, seq_index // 2
    hidden_units = grad_ffnkey.shape[1]
    keyin_part = after(outer_back(grad_hidden, keys_low), grad_ffnkey, grad_ffnvalue)
    grad_ffnkey, grad_ffnvalue = lax.psum((grad_ffnkey, grad_ffnvalue), "seq")
    grad_keyin = line_sum(keyin_part, 1)
    carry_two = grad_keyin * lagged_blend_coeffs[6]
    grad_normed_two = (
        grad_keyin
        - carry_two
        + jnp.concatenate([carry_two[1:], from_after(carry_two[:1], is_first, stride)], axis=0)
    )
    grad_attended, grad_gain_two, grad_bias_two = second_pull(grad_normed_two)
    grad_attended = grad_attended + grad_result
    grad_attended_low = grad_attended.astype(jnp.bfloat16)
    grad_branch = outer_back(grad_attended_low, out_low)
    (
        state_local,
        steps,
        slope,
        grad_gate,
        acceptance_extra,
        address_extra,
        content_extra,
        sums_a,
    ) = local_call(
        backward_local_kernel,
        local_heads,
        [state_shape, steps_shape, lines, low_lines, lines, lines, lines, tiny],
        (grad_branch, outputs, read, pieces, acceptance_lines, *raw_lines)
        + (widened_lines[1], widened_lines[2], earliest_tier_content, widened_lines[3])
        + (attention_scale_lines, attention_offset_lines, reward_row),
    )
    later_locals = jnp.stack([passed_along(state_local, "seq", -far * stride) for far in distances])
    (
        grad_state_in,
        grad_rec_low,
        grad_key_low,
        grad_value_low,
        grad_up_w,
        grad_up_a,
        grad_up_v,
        grad_first,
        sums_b,
    ) = local_call(
        backward_state_kernel,
        local_heads,
        [state_shape] + [low_lines] * 6 + [lines, tiny],
        (later_moves, later_locals, later_flags, states, pieces, steps, solved, wide, fixed)
        + (pair_rb, pair_rk, pair_ak, slope, acceptance_extra, address_extra, content_extra)
        + (acceptance_lines, *raw_lines, *widened_lines[:3], earliest_tier_content)
        + (attention_scale_lines, attention_offset_lines, forget_row),
    )
    grad_state_in = jnp.swapaxes(grad_state_in.reshape(HEAD_SIZE, local_heads, HEAD_SIZE), 0, 1)
    grad_headgain = jnp.concatenate([sums_b[0:2], sums_a[0:1]], axis=0)
    grad_headbias = jnp.concatenate([sums_b[2:4], sums_a[1:2]], axis=0)
    reward_loss_slope = sums_a[2]
    grad_decay = sums_b[4]
    grad_lift_low = [grad_up_w, grad_up_a, grad_up_v, grad_gate]
    square_grads = jnp.stack(
        [
            inner_rows(mixes[0], grad_rec_low),
            inner_rows(mixes[2], grad_key_low),
            inner_rows(mixes[3], grad_value_low),
            inner_rows(grad_attended_low, adapter_result),
        ]
    )
    grad_up = jnp.concatenate(
        [inner_rows(acts[index], grad_lift_low[index]) for index in range(4)], axis=0
    )
    split_grads = (
        outer_back(grad_rec_low, weights[0]),
        outer_back(grad_key_low, weights[1]),
        outer_back(grad_value_low, weights[2]),
    )
    split_ids = (0, 2, 3)
    norm_part = sum(
        (split_grads[index] * (1.0 - lagged_blend_coeffs[split_ids[index]]) for index in range(3))
    )
    prev_part = sum(
        (split_grads[index] * lagged_blend_coeffs[split_ids[index]] for index in range(3))
    )
    shift_part = jnp.stack([jnp.sum(item * delta, axis=0) for item in split_grads])
    acts_part = jnp.concatenate(
        [
            outer_back(
                grad_lift_low[index], up_matrix[sequence_spans[index][0] : sequence_spans[index][1]]
            )
            for index in range(4)
        ],
        axis=1,
    )
    spare = (-acts_part.shape[1]) % 128
    shift_columns = shift_part.size // overall_tally
    acts_packed = jnp.concatenate(
        [
            acts_part,
            shift_part.reshape(overall_tally, shift_columns),
            jnp.zeros((overall_tally, spare - shift_columns), F32),
        ],
        axis=1,
    )
    normed_part = norm_part + jnp.concatenate(
        [prev_part[1:], from_after(prev_part[:1], is_first, stride)], axis=0
    )
    acts_packed = line_sum(jnp.concatenate([acts_packed, normed_part], axis=1), 2)
    norm_sum = acts_packed[:, -EMBED_SIZE:]
    acts_sum = acts_packed[:, : acts_part.shape[1]]
    shift_sum = acts_packed[:, acts_part.shape[1] : acts_part.shape[1] + shift_columns]
    shift_sum = shift_sum.reshape(shift_part.shape)
    act_grads = [acts_sum[:, start_index:stop_index] for start_index, stop_index in sequence_spans]
    grad_hidden_low = [
        (act_grads[0] * (1.0 - tanh_w * tanh_w)).astype(jnp.bfloat16),
        act_grads[1].astype(jnp.bfloat16),
        act_grads[2].astype(jnp.bfloat16),
        (act_grads[3] * gate_sig * (1.0 - gate_sig)).astype(jnp.bfloat16),
    ]
    grad_down = jnp.concatenate(
        [inner_rows(grad_hidden_low[index], mixes[sources[index]]) for index in range(4)], axis=0
    )
    rep_grads = [
        outer_back(
            grad_hidden_low[index],
            down_matrix[:, sequence_spans[index][0] : sequence_spans[index][1]],
        )
        for index in range(4)
    ]
    grad_normed = norm_sum + sum(
        (rep_grads[index] * (1.0 - lagged_blend_coeffs[sources[index]]) for index in range(4))
    )
    grad_prev = sum(
        (rep_grads[index] * lagged_blend_coeffs[sources[index]] for index in range(4))
    )
    grad_normed = grad_normed + jnp.concatenate(
        [grad_prev[1:], from_after(grad_prev[:1], is_first, stride)], axis=0
    )
    grad_inputs, grad_gain_one, grad_bias_one = first_pull(grad_normed)
    tokens_grad = grad_attended + grad_inputs
    rep_shift = [jnp.sum(item * delta, axis=0) for item in rep_grads]
    grad_shift = jnp.stack(
        [
            shift_sum[0],
            rep_shift[0],
            shift_sum[1],
            shift_sum[2] + rep_shift[2],
            rep_shift[1],
            rep_shift[3],
            jnp.sum(grad_keyin * delta_two, axis=0),
        ]
    )
    choose = ((lax.iota(jnp.int32, stride) == sequence_id) & is_first).astype(jnp.float32)
    state_part = choose[:, None, None, None] * grad_state_in[None]
    small = (
        grad_shift,
        grad_down,
        grad_up,
        grad_headgain,
        grad_headbias,
        reward_loss_slope,
        grad_decay,
        state_part,
        jnp.stack([grad_gain_one, grad_gain_two, grad_bias_one, grad_bias_two]),
    )
    half_rows = EMBED_SIZE // 2
    square_parts = square_grads.reshape(4, 2, half_rows, width)
    square_parts = jnp.pad(square_parts, ((0, pairs - 4), (0, 0), (0, 0), (0, 0)))
    total_size = sum(item.size for item in small)
    padding = -total_size % (16 * pairs * width)
    packed = jnp.concatenate([item.reshape(-1) for item in small] + [jnp.zeros((padding,), F32)])
    packed = packed.reshape(pairs, 2, -1, width)
    moved_ffnkey = DECAY_KEEP * feedforward_address_velocity + grad_ffnkey
    moved_ffnvalue = DECAY_KEEP * feedforward_content_velocity + grad_ffnvalue
    which_wide = pair % 2
    part_index = (pair // 2) * 2 + core
    gram_part = gram_rows(which_wide, part_index, pairs, moved_ffnkey, moved_ffnvalue)
    own_part, gram_part = reduce_and_sum(
        jnp.concatenate([square_parts, packed], axis=2), gram_part, 3
    )
    own_velocity = jnp.concatenate([readin_velocity, emission_velocity.T[None]], axis=0)
    own_velocity = lax.dynamic_slice(
        own_velocity, (jnp.minimum(pair, 3), core * half_rows, 0), (1, half_rows, width)
    )
    own_square = own_part[:half_rows] + DECAY_KEEP * own_velocity[0]
    packed, whole_square, wide_gram = share_gather(own_square, own_part[half_rows:], gram_part, 5)
    wide_gram = wide_gram.reshape(EMBED_SIZE, EMBED_SIZE)
    moved_squares = to_all_pairs(after(own_square, whole_square), pairs)[:4]
    moved_squares = pair_whole(moved_squares, core).swapaxes(0, 1).reshape(4, EMBED_SIZE, width)
    packed = packed.reshape(-1)
    unpacked, place_in = [], 0
    for item in small:
        unpacked.append(packed[place_in : place_in + item.size].reshape(item.shape))
        place_in += item.size
    state_total, norm_gains = unpacked[7:]
    learnable_tensors = (
        lagged_blend_coeffs,
        standardize_scales,
        standardize_offsets,
        adapter_narrowing_coeffs,
        adapter_widening_coeffs,
        attention_scale_lines,
        attention_offset_lines,
        present_reward_array,
        forgetting_offset,
        readin_maps,
        emission_coeffs,
        feedforward_address_coeffs,
        feedforward_content_coeffs,
    )
    velocity_collection = (
        lagged_blend_velocity,
        standardize_scale_velocity,
        standardize_offset_velocity,
        narrowing_velocity,
        widening_velocity,
        attention_scale_velocity,
        attention_offset_velocity,
        reward_velocity_array,
        forgetting_velocity,
        readin_velocity,
        emission_velocity,
        feedforward_address_velocity,
        feedforward_content_velocity,
    )
    sink_moved = DECAY_KEEP * narrowing_velocity.T + unpacked[1]
    moved_rows = [
        DECAY_KEEP * lagged_blend_velocity + unpacked[0],
        DECAY_KEEP * standardize_scale_velocity + norm_gains[:2],
        DECAY_KEEP * standardize_offset_velocity + norm_gains[2:],
        sink_moved.T,
    ]
    moved_rows += [
        DECAY_KEEP * velocity + grad for velocity, grad in zip(velocity_collection[4:9], unpacked[2:7])
    ]
    moved_rows += [moved_squares[:3], moved_squares[3].T, moved_ffnkey, moved_ffnvalue]
    next_values = list(learnable_tensors)
    for index in (0, 1, 2, 5, 6, 7, 8):
        next_values[index] = vector_step(learnable_tensors[index], moved_rows[index])
    lift_moved = moved_rows[4]
    total_rank = lift_moved.shape[0]
    rank_pad = -total_rank % 128
    group = jnp.stack(
        [(lax.iota(jnp.int32, total_rank) >= edge).astype(jnp.int32) for edge in sequence_edges[1:4]]
    ).sum(axis=0)
    member = jnp.pad((group[:, None] == group[None, :]).astype(F32), ((0, rank_pad), (0, rank_pad)))
    rank_gram = jnp.pad(exact(lift_moved, lift_moved.T), ((0, rank_pad), (0, rank_pad)))
    lift_gram = lax.psum(rank_gram, "head")
    result_sum = lax.psum(after(product(activated, values_low), lift_gram), "head")
    block_output = ((attended + result_sum) * live).astype(jnp.bfloat16)
    sink_gram = jnp.pad(exact(sink_moved, sink_moved.T), ((0, rank_pad), (0, rank_pad)))
    rank_gram = jnp.where(core == 0, lift_gram, sink_gram)[None]
    wide_role = jnp.where((core == 1) & (pair < 4), 1 + which_wide, 0)
    wide_done = newton_wide(wide_role, wide_gram, moved_ffnkey, moved_ffnvalue)
    square_done = newton_square((core == 0) & (pair < 4), after(whole_square, wide_done))
    maps = newton_small(core >= 0, after(rank_gram, square_done, moved_squares, result_sum), member)
    square_done, maps, wide_done = lax.optimization_barrier((square_done, maps, wide_done))
    maps = pair_whole(maps[0], core)[:, :total_rank, :total_rank]
    lift_done = close(maps[0], lift_moved)
    sink_done = close(maps[1], sink_moved)
    head_index = lax.axis_index("head")
    square_done = lax.dynamic_slice_in_dim(square_done, head_index * width, width, 1)
    share = EMBED_SIZE // seq_count
    start_row = seq_index * share
    square_rows = lax.all_to_all(
        square_done.reshape(seq_count, share, width), "seq", 0, 0, tiled=True
    )[0:8:2]
    group_size = seq_count // 2
    wide_shares = wide_done.reshape(seq_count, share, hidden_units)
    rounds = []
    for step in range(group_size):
        chosen = jnp.where(pair % 2 == 0, step, (step + group_size // 2) % group_size)
        sent = lax.dynamic_index_in_dim(
            wide_shares, (pair // 2) * group_size + chosen, 0, keepdims=False
        )
        routes = []
        for half in range(2):
            origin = (1, 3) if half == 0 else (5, 7)
            routes.append((origin[0], half * group_size + step))
            routes.append((origin[1], half * group_size + (step + group_size // 2) % group_size))
        rounds.append(lax.ppermute(sent, "seq", routes))
    rounds = jnp.stack(rounds)
    in_group = seq_index % group_size
    wide_rows = [
        lax.dynamic_index_in_dim(rounds, in_group, 0, keepdims=False),
        lax.dynamic_index_in_dim(rounds, (in_group + group_size // 2) % group_size, 0, keepdims=False),
    ]
    rows_of = lambda item, axis: lax.dynamic_slice_in_dim(item, start_row, share, axis)
    next_values[9] = rows_of(readin_maps, 1) - ORTHO_STEP_RATE * square_rows[:3]
    next_values[10] = rows_of(emission_coeffs, 1) - ORTHO_STEP_RATE * square_rows[3].T
    next_values[11] = rows_of(feedforward_address_coeffs, 0) - ORTHO_STEP_RATE * wide_rows[0]
    next_values[12] = (
        rows_of(feedforward_content_coeffs, 1)
        - ORTHO_STEP_RATE * math.sqrt(max(1.0, FF / EMBED_SIZE)) * wide_rows[1].T
    )
    next_values[4] = adapter_widening_coeffs - ORTHO_STEP_RATE * lift_done
    next_values[3] = adapter_narrowing_coeffs - ORTHO_STEP_RATE * jnp.concatenate(
        [
            math.sqrt(max(1.0, EMBED_SIZE / (stop_index - start_index)))
            * sink_done[start_index:stop_index].T
            for start_index, stop_index in sequence_spans
        ],
        axis=1,
    )
    return (
        block_output,
        tokens_grad,
        grad_first,
        state_total,
        next_values[0],
        next_values[1],
        next_values[2],
        next_values[3],
        next_values[4],
        next_values[5],
        next_values[6],
        next_values[7],
        next_values[8],
        next_values[9],
        next_values[10],
        next_values[11],
        next_values[12],
        moved_rows[0],
        moved_rows[1],
        moved_rows[2],
        moved_rows[3],
        moved_rows[4],
        moved_rows[5],
        moved_rows[6],
        moved_rows[7],
        moved_rows[8],
        moved_rows[9],
        moved_rows[10],
        moved_rows[11],
        moved_rows[12],
    )


def solution(mesh):
    return jax.shard_map(
        on_device,
        mesh=mesh,
        in_specs=(
            P("seq", None),
            P("seq", None),
            P("seq", "head"),
            P(None, "head", None, None),
            P(),
            P(),
            P(),
            P(),
            P(),
            P(None, "head"),
            P(None, "head"),
            P(None, "head"),
            P("head"),
            P("head"),
            P(None, None, "head"),
            P("head", None),
            P(None, "head"),
            P("head", None),
            P(),
            P(),
            P(),
            P(),
            P(None, "head"),
            P(None, "head"),
            P(None, "head"),
            P("head"),
            P("head"),
            P(None, None, "head"),
            P("head", None),
            P(None, "head"),
            P("head", None),
        ),
        out_specs=(
            P("seq", None),
            P("seq", None),
            P("seq", "head"),
            P(None, "head", None, None),
            P(),
            P(),
            P(),
            P(),
            P(None, "head"),
            P(None, "head"),
            P(None, "head"),
            P("head"),
            P("head"),
            P(None, "seq", "head"),
            P("head", "seq"),
            P("seq", "head"),
            P("head", "seq"),
            P(),
            P(),
            P(),
            P(),
            P(None, "head"),
            P(None, "head"),
            P(None, "head"),
            P("head"),
            P("head"),
            P(None, None, "head"),
            P("head", None),
            P(None, "head"),
            P("head", None),
        ),
        check_vma=False,
    )
```
